32 devices in a mesh: seq: 4 (over z), chan: 8 (over y, x, core).
Axes of the slice: x: 2, y: 2, z: 4, core: 2. Of those that a mesh axis runs over, the one named last changes fastest.
Arguments:
- tokens: bfloat16 [2048, 4096], P('seq', 'chan'), may hold values from -6 to 6
- gate_proj: bfloat16 [4096, 8192], P(None, 'chan'), may hold values from -0.09375 to 0.09375
- value_proj: bfloat16 [4096, 8192], P(None, 'chan'), may hold values from -0.09375 to 0.09375
- state_proj: bfloat16 [4096, 256], replicated, may hold values from -0.0078125 to 0.0078125
- step_proj: bfloat16 [4096, 64], P(None, 'chan'), may hold values from -0.09375 to 0.09375
- step_bias: float32 [64], P('chan'), may hold values from -1 to 1
- decay_rate: float32 [64], P('chan'), may hold values from 0.0001 to 0.05
- skip_gain: float32 [64], P('chan'), may hold values from 0.5 to 4
- conv_kernel: float32 [4, 8192], P(None, 'chan'), may hold values from -3 to 3
- norm_gain: float32 [8192], P('chan'), may hold values from 0.1 to 1.9
- out_proj: bfloat16 [8192, 4096], P('chan'), may hold values from -0.046875 to 0.046875
- complement: int32 [4096], replicated, may hold values from 0 to 4095, as said below
- keep_mask: int32 [2048, 4096], P('seq', 'chan'), may hold values 0 or 1
Outputs:
- mixed: bfloat16 [2048, 4096], P('seq', 'chan')
The draws below stay inside these ranges and needn't reach their ends.
Inputs may be any that keep to these rules, and one draw needn't show every extreme that they name: complement pairs the features: complement[complement[j]] = j and complement[j] != j for every j.
All inputs are finite; a program needn't handle non-finite values. No bound on the sum of `keep_mask` on one device may be relied on, other than what follows from the above.
Results may differ from the reference program's by a relative error of at most 0.025.
Values may be sent and summed in bfloat16 or wider, within the bound.
A program may use at most 128 MiB of HBM per device.

```python
import math
import jax
import jax.numpy as jnp
from jax import lax

D = 4096
H = 64
P_SIZE = 128
N = 128
KW = 4
BLOCK = 256
DI = 8192
TOKENS = 2048


def draw_complement(key, part):
    order = jax.random.permutation(jax.random.fold_in(key, 17), jnp.arange(D, dtype=jnp.int32))
    pairs = order.reshape(D // 2, 2)
    paired = jnp.zeros((D,), jnp.int32).at[pairs[:, 0]].set(pairs[:, 1])
    paired = paired.at[pairs[:, 1]].set(pairs[:, 0])
    return paired


def set_ends(result, own_key, low, largest):
    place = [jax.random.randint(jax.random.fold_in(own_key, axis), (), 0, length) for axis, length in enumerate(result.shape)]
    longest = result.shape.index(max(result.shape))
    neighbour = place[:longest] + [(place[longest] + 1) % result.shape[longest]] + place[longest + 1:]
    return result.at[tuple(place)].set(low).at[tuple(neighbour)].set(largest)


def block_scale(own_key, dims, split, smallest, high):
    loudness, own = 1.0, jax.random.fold_in(own_key, 6)
    for dim, shards_of in split:
        heights = jnp.exp(jax.random.uniform(jax.random.fold_in(own, dim), (shards_of,), jnp.float32, smallest / len(split), high / len(split)))
        loudness = loudness * jnp.repeat(heights, dims[dim] // shards_of).reshape([-1 if axis == dim else 1 for axis in range(len(dims))])
    return loudness


def normal_values(stream_key, dims, width, reach, cuts=(), kind=jnp.bfloat16):
    drawn = width * jax.random.normal(stream_key, dims, jnp.float32)
    if cuts:
        drawn = drawn * block_scale(stream_key, dims, cuts, -0.22, 0.18)
    return jnp.clip(drawn, -reach, reach).astype(kind)


def setup_inputs(seed: int = 0) -> dict:
    key_of = jax.random.split(jax.random.key(seed), 14)
    tokens = normal_values(key_of[0], (TOKENS, D), 1.0, 6.0, ((0, 4), (1, 8)))
    gate_proj = normal_values(key_of[1], (D, DI), D ** -0.5, 0.09375, ((1, 8),))
    value_proj = normal_values(key_of[2], (D, DI), D ** -0.5, 0.09375, ((1, 8),))
    state_proj = normal_values(key_of[3], (D, 2 * N), (D * N) ** -0.5, 0.0078125)
    step_proj = normal_values(key_of[4], (D, H), D ** -0.5, 0.09375, ((1, 8),))
    step_bias = jnp.clip(jax.random.uniform(key_of[5], (H,), jnp.float32, -1.0, 1.0) * block_scale(key_of[5], (H,), ((0, 8),), -0.4, 0.0), -1.0, 1.0)
    decay_rate = jnp.clip(jnp.exp(math.log(0.05) - 6.214608 * jax.random.uniform(key_of[6], (H,), jnp.float32) ** block_scale(key_of[6], (H,), ((0, 8),), -0.2, 0.2)), 0.0001, 0.05)
    skip_gain = jnp.clip(jnp.exp(math.log(4.0) - 2.0794415 * jax.random.uniform(key_of[7], (H,), jnp.float32) ** block_scale(key_of[7], (H,), ((0, 8),), -0.2, 0.2)), 0.5, 4.0)
    conv_kernel = normal_values(key_of[8], (KW, DI), 0.5, 3.0, ((1, 8),), jnp.float32)
    norm_gain = jnp.clip(1.0 + 0.18 * jax.random.normal(key_of[9], (DI,), jnp.float32), 0.1, 1.9)
    out_proj = normal_values(key_of[10], (DI, D), (2 * H * P_SIZE) ** -0.5, 0.046875, ((0, 8),))
    complement = draw_complement(jax.random.fold_in(key_of[13], 71), 0)
    keep_mask = set_ends((jax.random.randint(key_of[12], (TOKENS, D), 0, 10) < 9).astype(jnp.int32), jax.random.fold_in(key_of[12], 1), 0, 1)
    return dict(tokens=tokens, gate_proj=gate_proj, value_proj=value_proj, state_proj=state_proj, step_proj=step_proj, step_bias=step_bias, decay_rate=decay_rate, skip_gain=skip_gain, conv_kernel=conv_kernel, norm_gain=norm_gain, out_proj=out_proj, complement=complement, keep_mask=keep_mask)


def block_step(state, items):
    x_heads, b_part, c_part, step, log_decay = items
    cumulative = jnp.cumsum(log_decay, axis=1)
    gaps = cumulative[:, :, None, :] - cumulative[:, None, :, :]
    length = cumulative.shape[1]
    lower_mask = (jnp.arange(length)[:, None] >= jnp.arange(length)[None, :])[None, :, :, None]
    weights = jnp.where(lower_mask, jnp.exp(jnp.where(lower_mask, gaps, 0.0)), 0.0)
    x_float = x_heads.astype(jnp.float32)
    b_float = b_part.astype(jnp.float32)
    c_float = c_part.astype(jnp.float32)
    highest = lax.Precision.HIGHEST
    scores = jnp.einsum('btn,bsn->bts', c_float, b_float, precision=highest)
    mixing = weights * scores[..., None] * step[:, None, :, :]
    inner_y = jnp.einsum('btsh,bshp->bthp', mixing, x_float, precision=highest)
    carried = jnp.exp(cumulative)[..., None] * jnp.einsum('btn,bhpn->bthp', c_float, state, precision=highest)
    total_decay = cumulative[:, -1, :]
    towards = jnp.exp(total_decay[:, None, :] - cumulative) * step
    fresh = jnp.einsum('bsh,bshp,bsn->bhpn', towards, x_float, b_float, precision=highest)
    new_state = jnp.exp(total_decay)[:, :, None, None] * state + fresh
    return (new_state, inner_y + carried)

def ssd_blocks(x_heads, b_part, c_part, step, log_decay):
    branches, length, heads, head_dim = x_heads.shape
    nblocks = length // BLOCK

    def blocked(arr):
        return jnp.moveaxis(arr.reshape((branches, nblocks, BLOCK) + arr.shape[2:]), 1, 0)
    start_state = jnp.zeros((branches, heads, head_dim, b_part.shape[-1]), jnp.float32)
    end_state, outputs = lax.scan(block_step, start_state, (blocked(x_heads), blocked(b_part), blocked(c_part), blocked(step), blocked(log_decay)))
    return (jnp.moveaxis(outputs, 0, 1).reshape(x_heads.shape), end_state)

def reference(tokens, gate_proj, value_proj, state_proj, step_proj, step_bias, decay_rate, skip_gain, conv_kernel, norm_gain, out_proj, complement, keep_mask):
    inner = gate_proj.shape[1]
    heads = step_proj.shape[1]
    head_dim = inner // heads
    nstate = state_proj.shape[1] // 2
    length = tokens.shape[0]

    def project(inputs):
        gate_part = jnp.dot(inputs, gate_proj, preferred_element_type=jnp.float32).astype(jnp.bfloat16)
        value_part = jnp.dot(inputs, value_proj, preferred_element_type=jnp.float32).astype(jnp.bfloat16)
        state_part = jnp.dot(inputs, state_proj, preferred_element_type=jnp.float32).astype(jnp.bfloat16)
        step_raw = jnp.dot(inputs, step_proj, preferred_element_type=jnp.float32)
        return (gate_part, value_part, state_part, step_raw)
    forward = project(tokens)
    reverse = project(jnp.take(tokens, complement, axis=1)[::-1])
    gate_part, value_part, state_part, step_raw = [jnp.stack([a, b]) for a, b in zip(forward, reverse)]
    padded = jnp.concatenate([jnp.zeros((2, KW - 1, inner), jnp.float32), value_part.astype(jnp.float32)], axis=1)
    conv = conv_kernel[0] * padded[:, 0:length, :]
    for tap in range(1, KW):
        conv = conv + conv_kernel[tap] * padded[:, tap:tap + length, :]
    x_ssm = jax.nn.silu(conv).astype(jnp.bfloat16)
    step = jax.nn.softplus(step_raw + step_bias)
    log_decay = -step * decay_rate
    x_heads = x_ssm.reshape(2, length, heads, head_dim)
    local_y, end_state = ssd_blocks(x_heads, state_part[..., :nstate], state_part[..., nstate:], step, log_decay)
    full_y = local_y + skip_gain[:, None] * x_heads.astype(jnp.float32)
    gated = full_y * jax.nn.silu(gate_part.astype(jnp.float32).reshape(2, length, heads, head_dim))
    scale = lax.rsqrt(lax.optimization_barrier(jnp.mean(gated * gated, axis=-1, keepdims=True)) + 1e-05)
    normed = (gated * scale * norm_gain.reshape(heads, head_dim)).reshape(2, length, inner).astype(jnp.bfloat16)
    stacked = jnp.concatenate([normed[0], normed[1][::-1]], axis=1)
    out_table = jnp.concatenate([out_proj, jnp.take(out_proj, complement, axis=1)], axis=0)
    total = jnp.dot(stacked, out_table, preferred_element_type=jnp.float32)
    return (total * keep_mask.astype(jnp.float32) * (1.0 / 0.9)).astype(jnp.bfloat16)
```

```python
import functools

import jax
import jax.numpy as jnp
from jax import lax
from jax.experimental import pallas as pl
from jax.experimental.pallas import tpu as pltpu
from jax.sharding import PartitionSpec as P

KW = 4
HALO = 16
TILE = 256
F32 = jnp.float32
BF16 = jnp.bfloat16
VMEM_LIMIT = 50 * 1024 * 1024


def params(grid_rank):
    return pltpu.CompilerParams(
        dimension_semantics=("arbitrary",) * grid_rank, vmem_limit_bytes=VMEM_LIMIT
    )


def permute_body(a_ref, partner_ref, out_ref):
    width = a_ref.shape[1]
    tile = out_ref.shape[1]
    depth = min(1024, width)
    total = jnp.zeros(out_ref.shape, F32)
    for low in range(0, width, depth):
        source = lax.broadcasted_iota(jnp.int32, (depth, tile), 0) + low
        chosen = jnp.where(source == partner_ref[...], 1.0, 0.0).astype(BF16)
        total += jnp.dot(a_ref[:, low : low + depth], chosen, preferred_element_type=F32)
    out_ref[...] = total.astype(BF16)


def permute_columns(a, partner):
    rows, width = a.shape
    tile = 512
    return pl.pallas_call(
        permute_body,
        grid=(width // tile,),
        in_specs=[
            pl.BlockSpec((rows, width), lambda j: (0, 0)),
            pl.BlockSpec((1, tile), lambda j: (0, j)),
        ],
        out_specs=pl.BlockSpec((rows, tile), lambda j: (0, j)),
        out_shape=jax.ShapeDtypeStruct((rows, width), BF16),
        compiler_params=params(1),
        cost_estimate=pl.CostEstimate(
            flops=2 * rows * width * width, bytes_accessed=4 * rows * width, transcendentals=0
        ),
    )(a, partner)


def column_of(ref, head):
    values = ref[...]
    lanes = lax.broadcasted_iota(jnp.int32, values.shape, 1)
    return jnp.sum(jnp.where(lanes == head, values, 0.0), axis=1, keepdims=True)


def state_body(value_ref, halo_ref, taps_ref, b_ref, step_ref, cum_ref, xs_ref, state_ref):
    branch, head = pl.program_id(0), pl.program_id(1)
    rows = value_ref.shape[0]
    nstate = b_ref.shape[1]
    value = value_ref[...].astype(F32)
    halo = halo_ref[...].astype(F32)
    step = column_of(step_ref, head)
    cum = column_of(cum_ref, head)

    def finish(conv, end):
        xs = (conv / (1.0 + jnp.exp(-conv))).astype(BF16)
        xs_ref[...] = xs
        weighted = (xs.astype(F32) * (jnp.exp(end - cum) * step)).astype(BF16)
        state = lax.dot_general(
            b_ref[...], weighted, (((0,), (0,)), ((), ())), preferred_element_type=F32
        )
        state_ref[0, 0, :nstate, :] = state.astype(BF16)
        state_ref[0, 0, nstate:, :] = jnp.broadcast_to(
            jnp.exp(end), (HALO, state.shape[1])
        ).astype(BF16)

    @pl.when(branch == 0)
    def _():
        ext = jnp.concatenate([halo, value], axis=0)
        conv = taps_ref[KW - 1 : KW, :] * value
        for k in range(KW - 1):
            low = HALO - (KW - 1) + k
            conv += taps_ref[k : k + 1, :] * ext[low : low + rows]
        finish(conv, cum[rows - 1 : rows])

    @pl.when(branch == 1)
    def _():
        ext = jnp.concatenate([value, halo], axis=0)
        conv = taps_ref[KW - 1 : KW, :] * value
        for k in range(KW - 1):
            low = KW - 1 - k
            conv += taps_ref[k : k + 1, :] * ext[low : low + rows]
        finish(conv, cum[0:1])


def local_body(skip_ref, xs_ref, b_ref, c_ref, cum_ref, step_row_ref, cum_row_ref, y_ref, scores):
    branch, head = pl.program_id(0), pl.program_id(1)
    rows = xs_ref.shape[0]

    @pl.when(head == 0)
    def _():
        scores[...] = lax.dot_general(
            c_ref[...], b_ref[...], (((1,), (1,)), ((), ())), preferred_element_type=F32
        )

    cum = column_of(cum_ref, head)
    cum_row = cum_row_ref[0]
    step_row = step_row_ref[0]
    xs = xs_ref[...]
    skip = skip_ref[head]
    size = min(TILE, rows)
    below = lax.broadcasted_iota(jnp.int32, (size, size), 0) - lax.broadcasted_iota(
        jnp.int32, (size, size), 1
    )

    def run(sign):
        for t in range(0, rows, size):
            at = slice(t, t + size)
            total = xs[at].astype(F32) * skip
            for s in range(0, rows, size):
                if sign * (t - s) < 0:
                    continue
                gaps = cum[at] - cum_row[:, s : s + size]
                if s == t:
                    gaps = jnp.where(sign * below >= 0, gaps, -jnp.inf)
                mixing = jnp.exp(gaps) * (scores[at, s : s + size] * step_row[:, s : s + size])
                total += jnp.dot(
                    mixing.astype(BF16), xs[s : s + size], preferred_element_type=F32
                )
            y_ref[at, :] = total

    @pl.when(branch == 0)
    def _():
        run(1)

    @pl.when(branch == 1)
    def _():
        run(-1)


def norm_body(y_ref, c_ref, cum_ref, gate_ref, gain_ref, enter_ref, out_ref):
    head = pl.program_id(1)
    cum = column_of(cum_ref, head)
    carried = jnp.dot(c_ref[...], enter_ref[0, 0], preferred_element_type=F32)
    y = y_ref[...] + jnp.exp(cum) * carried
    gate = gate_ref[...].astype(F32)
    gated = y * (gate / (1.0 + jnp.exp(-gate)))
    mean = jnp.mean(gated * gated, axis=1, keepdims=True)
    out_ref[...] = (gated * lax.rsqrt(mean + 1e-05) * gain_ref[...]).astype(BF16)


def shift(block, distance):
    count = lax.axis_size("seq")
    route = [(i, i + distance) for i in range(count) if 0 <= i + distance < count]
    return lax.ppermute(block, "seq", route)


def entering(packed, nstate):
    count = lax.axis_size("seq")
    place = lax.axis_index("seq")
    gathered = lax.all_gather(packed, "seq")
    ends = gathered[:, :, :, :nstate, :].astype(F32)
    decays = gathered[:, :, :, nstate : nstate + 1, :].astype(F32)
    ahead = jnp.zeros(ends.shape[2:], F32)
    for z in range(count):
        ahead = jnp.where(z < place, decays[z, 0] * ahead + ends[z, 0], ahead)
    behind = jnp.zeros(ends.shape[2:], F32)
    for z in reversed(range(count)):
        behind = jnp.where(z > place, decays[z, 1] * behind + ends[z, 1], behind)
    return jnp.stack([ahead, behind]).astype(BF16)


def shards(
    tokens,
    gate_proj,
    value_proj,
    state_proj,
    step_proj,
    step_bias,
    decay_rate,
    skip_gain,
    conv_kernel,
    norm_gain,
    out_proj,
    complement,
    keep_mask,
):
    rows = tokens.shape[0]
    inner = gate_proj.shape[1]
    heads = step_proj.shape[1]
    head_dim = inner // heads
    nstate = state_proj.shape[1] // 2
    partner = complement[None, :]
    half = rows // 2

    parts = [
        lax.all_gather(tokens[low : low + half], "chan", axis=1, tiled=True)
        for low in (0, half)
    ]
    out_perm = permute_columns(out_proj, partner)
    swapped = [permute_columns(part, partner) for part in parts]
    both = jnp.concatenate(parts + swapped, axis=0)

    def project(weights):
        return jnp.dot(both, weights, preferred_element_type=F32)

    value = project(value_proj).astype(BF16)
    halo = jnp.concatenate(
        [shift(value[rows - HALO : rows], 1), shift(value[rows : rows + HALO], -1)], axis=0
    )
    bc = project(state_proj).astype(BF16)
    step = jax.nn.softplus(project(step_proj) + step_bias).reshape(2, rows, heads)
    log_decay = -step * decay_rate
    cum = jnp.stack(
        [jnp.cumsum(log_decay[0], axis=0), lax.cumsum(log_decay[1], axis=0, reverse=True)]
    )
    step_rows = jnp.swapaxes(step, 1, 2).reshape(2 * heads, 1, rows)
    cum_rows = jnp.swapaxes(cum, 1, 2).reshape(2 * heads, 1, rows)
    step = step.reshape(2 * rows, heads)
    cum = cum.reshape(2 * rows, heads)
    gate = project(gate_proj).astype(BF16)

    grid = (2, heads)
    block = pl.BlockSpec((rows, head_dim), lambda b, h: (b, h))
    b_block = pl.BlockSpec((rows, nstate), lambda b, h: (b, 0))
    c_block = pl.BlockSpec((rows, nstate), lambda b, h: (b, 1))
    column = pl.BlockSpec((rows, heads), lambda b, h: (b, 0))
    row = pl.BlockSpec((1, 1, rows), lambda b, h: (b * heads + h, 0, 0))

    xs, packed = pl.pallas_call(
        state_body,
        grid=grid,
        in_specs=[
            block,
            pl.BlockSpec((HALO, head_dim), lambda b, h: (b, h)),
            pl.BlockSpec((KW, head_dim), lambda b, h: (0, h)),
            b_block,
            column,
            column,
        ],
        out_specs=[
            block,
            pl.BlockSpec((1, 1, nstate + HALO, head_dim), lambda b, h: (b, h, 0, 0)),
        ],
        out_shape=[
            jax.ShapeDtypeStruct((2 * rows, inner), BF16),
            jax.ShapeDtypeStruct((2, heads, nstate + HALO, head_dim), BF16),
        ],
        compiler_params=params(2),
    )(value, halo, conv_kernel, bc, step, cum)

    enter = entering(packed, nstate)

    y = pl.pallas_call(
        local_body,
        grid=grid,
        in_specs=[
            pl.BlockSpec(memory_space=pltpu.SMEM),
            block,
            b_block,
            c_block,
            column,
            row,
            row,
        ],
        out_specs=block,
        out_shape=jax.ShapeDtypeStruct((2 * rows, inner), F32),
        scratch_shapes=[pltpu.VMEM((rows, rows), F32)],
        compiler_params=params(2),
        cost_estimate=pl.CostEstimate(
            flops=8 * rows * rows * inner,
            bytes_accessed=16 * rows * inner,
            transcendentals=2 * heads * rows * rows,
        ),
    )(skip_gain, xs, bc, bc, cum, step_rows, cum_rows)

    normed = pl.pallas_call(
        norm_body,
        grid=grid,
        in_specs=[
            block,
            c_block,
            column,
            block,
            pl.BlockSpec((1, head_dim), lambda b, h: (0, h)),
            pl.BlockSpec((1, 1, nstate, head_dim), lambda b, h: (b, h, 0, 0)),
        ],
        out_specs=pl.BlockSpec((rows, head_dim), lambda b, h: (0, b * heads + h)),
        out_shape=jax.ShapeDtypeStruct((rows, 2 * inner), BF16),
        compiler_params=params(2),
    )(y, bc, cum, gate, norm_gain[None, :], enter)

    table = jnp.concatenate([out_proj, out_perm], axis=0)
    results = []
    for low in (0, half):
        partial = jnp.dot(normed[low : low + half], table, preferred_element_type=F32)
        summed = lax.psum_scatter(
            partial.astype(BF16), "chan", scatter_dimension=1, tiled=True
        ).astype(F32)
        kept = keep_mask[low : low + half].astype(F32)
        results.append((summed * kept * (1.0 / 0.9)).astype(BF16))
    return jnp.concatenate(results, axis=0)


def solution(mesh):
    return jax.shard_map(
        shards,
        mesh=mesh,
        in_specs=(
            P("seq", "chan"),
            P(None, "chan"),
            P(None, "chan"),
            P(),
            P(None, "chan"),
            P("chan"),
            P("chan"),
            P("chan"),
            P(None, "chan"),
            P("chan"),
            P("chan", None),
            P(),
            P("seq", "chan"),
        ),
        out_specs=P("seq", "chan"),
        check_vma=False,
    )
```

```python
import functools

import jax
import jax.numpy as jnp
from jax import lax
from jax.experimental import pallas as pl
from jax.experimental.pallas import tpu as pltpu
from jax.sharding import PartitionSpec as P

KW = 4
HALO = 16
TILE = 256
DEPTH = 256
MESH = pl.DeviceIdType.MESH
F32 = jnp.float32
BF16 = jnp.bfloat16
VMEM_LIMIT = 50 * 1024 * 1024


def params(grid_rank):
    return pltpu.CompilerParams(
        dimension_semantics=("arbitrary",) * grid_rank, vmem_limit_bytes=VMEM_LIMIT
    )


def chosen_rows(partner, low, depth):
    local = jnp.clip(partner - low, -1, depth).astype(F32).astype(BF16)
    source = lax.broadcasted_iota(jnp.int32, (depth, partner.shape[1]), 0)
    source = source.astype(F32).astype(BF16)
    return jnp.where(source == local, jnp.ones((), BF16), jnp.zeros((), BF16))


def permute_body(a_ref, partner_ref, out_ref):
    width = a_ref.shape[1]
    total = jnp.zeros(out_ref.shape, F32)
    for low in range(0, width, DEPTH):
        chosen = chosen_rows(partner_ref[...], low, DEPTH)
        total += jnp.dot(a_ref[:, low : low + DEPTH], chosen, preferred_element_type=F32)
    out_ref[...] = total.astype(BF16)


def permute_columns(a, partner):
    rows, width = a.shape
    tile = 512
    return pl.pallas_call(
        permute_body,
        grid=(width // tile,),
        in_specs=[
            pl.BlockSpec((rows, width), lambda j: (0, 0)),
            pl.BlockSpec((1, tile), lambda j: (0, j)),
        ],
        out_specs=pl.BlockSpec((rows, tile), lambda j: (0, j)),
        out_shape=jax.ShapeDtypeStruct((rows, width), BF16),
        compiler_params=params(1),
        cost_estimate=pl.CostEstimate(
            flops=2 * rows * width * width, bytes_accessed=4 * rows * width, transcendentals=0
        ),
    )(a, partner)


def column_of(ref, head):
    values = ref[...]
    lanes = lax.broadcasted_iota(jnp.int32, values.shape, 1)
    return jnp.sum(jnp.where(lanes == head, values, 0.0), axis=1, keepdims=True)


def state_body(value_ref, halo_ref, taps_ref, b_ref, step_ref, cum_ref, xs_ref, state_ref):
    branch, head = pl.program_id(0), pl.program_id(1)
    rows = value_ref.shape[0]
    nstate = b_ref.shape[1]
    value = value_ref[...].astype(F32)
    halo = halo_ref[...].astype(F32)
    step = column_of(step_ref, head)
    cum = column_of(cum_ref, head)

    def finish(conv, end):
        xs = (conv / (1.0 + jnp.exp(-conv))).astype(BF16)
        xs_ref[...] = xs
        weighted = (xs.astype(F32) * (jnp.exp(end - cum) * step)).astype(BF16)
        state = lax.dot_general(
            b_ref[...], weighted, (((0,), (0,)), ((), ())), preferred_element_type=F32
        )
        state_ref[0, 0, :nstate, :] = state.astype(BF16)
        state_ref[0, 0, nstate:, :] = jnp.broadcast_to(
            jnp.exp(end), (HALO, state.shape[1])
        ).astype(BF16)

    @pl.when(branch == 0)
    def _():
        ext = jnp.concatenate([halo, value], axis=0)
        conv = taps_ref[KW - 1 : KW, :] * value
        for k in range(KW - 1):
            low = HALO - (KW - 1) + k
            conv += taps_ref[k : k + 1, :] * ext[low : low + rows]
        finish(conv, cum[rows - 1 : rows])

    @pl.when(branch == 1)
    def _():
        ext = jnp.concatenate([value, halo], axis=0)
        conv = taps_ref[KW - 1 : KW, :] * value
        for k in range(KW - 1):
            low = KW - 1 - k
            conv += taps_ref[k : k + 1, :] * ext[low : low + rows]
        finish(conv, cum[0:1])


def local_body(skip_ref, xs_ref, b_ref, c_ref, cum_ref, step_row_ref, cum_row_ref, y_ref, scores):
    branch, head = pl.program_id(0), pl.program_id(1)
    rows = xs_ref.shape[0]

    @pl.when(head == 0)
    def _():
        scores[...] = lax.dot_general(
            c_ref[...], b_ref[...], (((1,), (1,)), ((), ())), preferred_element_type=F32
        )

    cum = column_of(cum_ref, head)
    cum_row = cum_row_ref[0]
    step_row = step_row_ref[0]
    xs = xs_ref[...]
    skip = skip_ref[head]
    size = min(TILE, rows)
    below = lax.broadcasted_iota(jnp.int32, (size, size), 0) - lax.broadcasted_iota(
        jnp.int32, (size, size), 1
    )

    def run(sign):
        for t in range(0, rows, size):
            at = slice(t, t + size)
            total = xs[at].astype(F32) * skip
            for s in range(0, rows, size):
                if sign * (t - s) < 0:
                    continue
                gaps = cum[at] - cum_row[:, s : s + size]
                if s == t:
                    gaps = jnp.where(sign * below >= 0, gaps, -jnp.inf)
                mixing = jnp.exp(gaps) * (scores[at, s : s + size] * step_row[:, s : s + size])
                total += jnp.dot(
                    mixing.astype(BF16), xs[s : s + size], preferred_element_type=F32
                )
            y_ref[at, :] = total

    @pl.when(branch == 0)
    def _():
        run(1)

    @pl.when(branch == 1)
    def _():
        run(-1)


def norm_body(y_ref, c_ref, cum_ref, gate_ref, gain_ref, enter_ref, out_ref):
    head = pl.program_id(1)
    cum = column_of(cum_ref, head)
    carried = jnp.dot(c_ref[...], enter_ref[0, 0], preferred_element_type=F32)
    y = y_ref[...] + jnp.exp(cum) * carried
    gate = gate_ref[...].astype(F32)
    gated = y * (gate / (1.0 + jnp.exp(-gate)))
    mean = jnp.mean(gated * gated, axis=1, keepdims=True)
    out_ref[...] = (gated * lax.rsqrt(mean + 1e-05) * gain_ref[...]).astype(BF16)


def shift(block, distance):
    count = lax.axis_size("seq")
    route = [(i, i + distance) for i in range(count) if 0 <= i + distance < count]
    return lax.ppermute(block, "seq", route)


def chain_body(packed_ref, enter_ref, inbox, outbox, send_sem, recv_sem):
    heads = packed_ref.shape[1]
    nstate = inbox.shape[2]
    count = lax.axis_size("seq")
    place = lax.axis_index("seq")
    toward = [(place + 1) % count, (place + count - 1) % count]
    first = [place == 0, place == count - 1]
    last = [place == count - 1, place == 0]

    barrier = pltpu.get_barrier_semaphore()
    for branch in (0, 1):

        @pl.when(jnp.logical_not(last[branch]))
        def _(branch=branch):
            pl.semaphore_signal(
                barrier, inc=1, device_id={"seq": toward[branch]}, device_id_type=MESH
            )

    pl.semaphore_wait(barrier, jnp.where(place == 0, 0, 1) + jnp.where(place == count - 1, 0, 1))

    def copy(branch, head):
        return pltpu.make_async_remote_copy(
            src_ref=outbox.at[branch, head],
            dst_ref=inbox.at[branch, head],
            send_sem=send_sem.at[branch, head],
            recv_sem=recv_sem.at[branch, head],
            device_id={"seq": toward[branch]},
            device_id_type=MESH,
        )

    def relay(branch, head):
        copy(branch, head).wait_recv()
        arrived = inbox[branch, head]
        enter_ref[branch, head] = arrived

        @pl.when(jnp.logical_not(last[branch]))
        def _():
            decay = packed_ref[branch, head, nstate : nstate + 1, :].astype(F32)
            end = packed_ref[branch, head, :nstate, :].astype(F32)
            outbox[branch, head] = (decay * arrived.astype(F32) + end).astype(BF16)
            copy(branch, head).start()

    for branch in (0, 1):

        @pl.when(first[branch])
        def _(branch=branch):
            for head in range(heads):
                enter_ref[branch, head] = jnp.zeros(inbox.shape[2:], BF16)
                outbox[branch, head] = packed_ref[branch, head, :nstate, :]
                copy(branch, head).start()

    for head in range(heads):
        for branch in (0, 1):

            @pl.when(jnp.logical_not(first[branch]))
            def _(branch=branch, head=head):
                relay(branch, head)

    for branch in (0, 1):

        @pl.when(jnp.logical_not(last[branch]))
        def _(branch=branch):
            for head in range(heads):
                copy(branch, head).wait_send()


def entering(packed, nstate):
    _, heads, _, head_dim = packed.shape
    shape = (2, heads, nstate, head_dim)
    vmem = pl.BlockSpec(memory_space=pltpu.VMEM)
    return pl.pallas_call(
        chain_body,
        in_specs=[vmem],
        out_specs=vmem,
        out_shape=jax.ShapeDtypeStruct(shape, BF16),
        scratch_shapes=[
            pltpu.VMEM(shape, BF16),
            pltpu.VMEM(shape, BF16),
            pltpu.SemaphoreType.DMA((2, heads)),
            pltpu.SemaphoreType.DMA((2, heads)),
        ],
        compiler_params=pltpu.CompilerParams(
            collective_id=1, has_side_effects=True, vmem_limit_bytes=VMEM_LIMIT
        ),
    )(packed)


def flip(me, bit):
    return me + bit * (1 - 2 * ((me // bit) % 2))


def greet(partners):
    barrier = pltpu.get_barrier_semaphore()
    for partner in partners:
        pl.semaphore_signal(barrier, inc=1, device_id={"chan": partner}, device_id_type=MESH)
    pl.semaphore_wait(barrier, len(partners))


def output_body(
    normed_ref, table_ref, partner_ref, out_ref,
    reverse, total, mine, theirs, sent, diagonal, across,
    core_send, core_recv, chip_send, chip_recv,
):
    rows, width = reverse.shape
    inner = table_ref.shape[0]
    cols = out_ref.shape[1]
    half = rows // 2
    me = lax.axis_index("chan")
    mate, beside, above = flip(me, 1), flip(me, 2), flip(me, 4)
    greet((mate, beside, above))

    def at(block):
        return pl.ds(pl.multiple_of(block * cols, cols), cols)

    def project(block, carry):
        reverse[:, at(block)] = jnp.dot(
            normed_ref[:, inner:], table_ref[:, at(block)], preferred_element_type=F32
        ).astype(BF16)
        return carry

    lax.fori_loop(0, width // cols, project, 0)

    def remote(src, dst, send_sem, recv_sem, to):
        return pltpu.make_async_remote_copy(
            src_ref=src, dst_ref=dst, send_sem=send_sem, recv_sem=recv_sem,
            device_id={"chan": to}, device_id_type=MESH,
        )

    def core_copy(slot):
        return remote(
            mine.at[slot], theirs.at[slot], core_send.at[slot], core_recv.at[slot], mate
        )

    low, high = pl.ds(0, half), pl.ds(half, half)
    chip_copies = [
        remote(sent.at[0, low], diagonal.at[0], chip_send.at[0], chip_recv.at[0], beside),
        remote(sent.at[0, high], diagonal.at[1], chip_send.at[1], chip_recv.at[1], above),
        remote(sent.at[1, low], across.at[0, low], chip_send.at[2], chip_recv.at[2], beside),
        remote(sent.at[1, high], across.at[0, high], chip_send.at[3], chip_recv.at[3], beside),
        remote(sent.at[2, high], across.at[1, high], chip_send.at[4], chip_recv.at[4], above),
        remote(sent.at[2, low], across.at[1, low], chip_send.at[5], chip_recv.at[5], above),
    ]

    def stage(chip, carry):
        is_beside = (chip == 0) | (chip == 1)
        is_above = (chip == 0) | (chip == 2)
        base = jnp.where(is_beside, beside - me, 0) + jnp.where(is_above, above - me, 0) + me

        def compute(turn, inner_carry):
            block = jnp.where(turn == 0, flip(base, 1), base)
            partner = partner_ref[:, at(block)]
            part = jnp.dot(
                normed_ref[:, :inner], table_ref[:, at(block)], preferred_element_type=F32
            )
            for depth in range(0, width, DEPTH):
                part += jnp.dot(
                    reverse[:, depth : depth + DEPTH],
                    chosen_rows(partner, depth, DEPTH),
                    preferred_element_type=F32,
                )
            total[...] = part

            @pl.when(turn == 0)
            def _():
                mine[chip] = part.astype(BF16)
                core_copy(chip).start()

            return inner_carry

        lax.fori_loop(0, 2, compute, 0)
        core_copy(chip).wait_recv()
        total[...] += theirs[chip].astype(F32)

        @pl.when(chip == 0)
        def _():
            sent[0] = total[...].astype(BF16)
            chip_copies[0].start()
            chip_copies[1].start()

        @pl.when(chip == 1)
        def _():
            sent[1, :half] = total[:half].astype(BF16)
            chip_copies[2].start()
            chip_copies[1].wait_recv()
            sent[1, half:] = (total[half:] + diagonal[1].astype(F32)).astype(BF16)
            chip_copies[3].start()

        @pl.when(chip == 2)
        def _():
            sent[2, half:] = total[half:].astype(BF16)
            chip_copies[4].start()
            chip_copies[0].wait_recv()
            sent[2, :half] = (total[:half] + diagonal[0].astype(F32)).astype(BF16)
            chip_copies[5].start()

        return carry

    lax.fori_loop(0, 4, stage, 0)
    for copy in chip_copies[2:]:
        copy.wait_recv()
    out_ref[...] = total[...] + across[0].astype(F32) + across[1].astype(F32)
    for slot in range(4):
        core_copy(slot).wait_send()
    for copy in chip_copies:
        copy.wait_send()


def output_sum(normed, table, partner, cols):
    rows = normed.shape[0]
    width = table.shape[1]
    vmem = pl.BlockSpec(memory_space=pltpu.VMEM)
    block = (rows, cols)
    return pl.pallas_call(
        output_body,
        in_specs=[vmem] * 3,
        out_specs=vmem,
        out_shape=jax.ShapeDtypeStruct(block, F32),
        scratch_shapes=[
            pltpu.VMEM((rows, width), BF16),
            pltpu.VMEM(block, F32),
            pltpu.VMEM((4,) + block, BF16),
            pltpu.VMEM((4,) + block, BF16),
            pltpu.VMEM((3,) + block, BF16),
            pltpu.VMEM((2, rows // 2, cols), BF16),
            pltpu.VMEM((2,) + block, BF16),
            pltpu.SemaphoreType.DMA((4,)),
            pltpu.SemaphoreType.DMA((4,)),
            pltpu.SemaphoreType.DMA((6,)),
            pltpu.SemaphoreType.DMA((6,)),
        ],
        compiler_params=pltpu.CompilerParams(
            collective_id=2, has_side_effects=True, vmem_limit_bytes=VMEM_LIMIT
        ),
        cost_estimate=pl.CostEstimate(
            flops=2 * rows * width * (2 * table.shape[0] + width),
            bytes_accessed=2 * table.size + 2 * normed.size,
            transcendentals=0,
        ),
    )(normed, table, partner)


def shards(
    tokens,
    gate_proj,
    value_proj,
    state_proj,
    step_proj,
    step_bias,
    decay_rate,
    skip_gain,
    conv_kernel,
    norm_gain,
    out_proj,
    complement,
    keep_mask,
):
    rows = tokens.shape[0]
    inner = gate_proj.shape[1]
    heads = step_proj.shape[1]
    head_dim = inner // heads
    nstate = state_proj.shape[1] // 2
    partner = complement[None, :]
    half = rows // 2

    parts = [
        lax.all_gather(tokens[low : low + half], "chan", axis=1, tiled=True)
        for low in (0, half)
    ]
    swapped = [permute_columns(part, partner) for part in parts]
    both = jnp.concatenate(parts + swapped, axis=0)

    def project(weights):
        return jnp.dot(both, weights, preferred_element_type=F32)

    value = project(value_proj).astype(BF16)
    halo = jnp.concatenate(
        [shift(value[rows - HALO : rows], 1), shift(value[rows : rows + HALO], -1)], axis=0
    )
    bc = project(state_proj).astype(BF16)
    step = jax.nn.softplus(project(step_proj) + step_bias).reshape(2, rows, heads)
    log_decay = -step * decay_rate
    cum = jnp.stack(
        [jnp.cumsum(log_decay[0], axis=0), lax.cumsum(log_decay[1], axis=0, reverse=True)]
    )
    step_rows = jnp.swapaxes(step, 1, 2).reshape(2 * heads, 1, rows)
    cum_rows = jnp.swapaxes(cum, 1, 2).reshape(2 * heads, 1, rows)
    step = step.reshape(2 * rows, heads)
    cum = cum.reshape(2 * rows, heads)
    gate = project(gate_proj).astype(BF16)

    grid = (2, heads)
    block = pl.BlockSpec((rows, head_dim), lambda b, h: (b, h))
    b_block = pl.BlockSpec((rows, nstate), lambda b, h: (b, 0))
    c_block = pl.BlockSpec((rows, nstate), lambda b, h: (b, 1))
    column = pl.BlockSpec((rows, heads), lambda b, h: (b, 0))
    row = pl.BlockSpec((1, 1, rows), lambda b, h: (b * heads + h, 0, 0))

    xs, packed = pl.pallas_call(
        state_body,
        grid=grid,
        in_specs=[
            block,
            pl.BlockSpec((HALO, head_dim), lambda b, h: (b, h)),
            pl.BlockSpec((KW, head_dim), lambda b, h: (0, h)),
            b_block,
            column,
            column,
        ],
        out_specs=[
            block,
            pl.BlockSpec((1, 1, nstate + HALO, head_dim), lambda b, h: (b, h, 0, 0)),
        ],
        out_shape=[
            jax.ShapeDtypeStruct((2 * rows, inner), BF16),
            jax.ShapeDtypeStruct((2, heads, nstate + HALO, head_dim), BF16),
        ],
        compiler_params=params(2),
    )(value, halo, conv_kernel, bc, step, cum)

    enter = entering(packed, nstate)

    y = pl.pallas_call(
        local_body,
        grid=grid,
        in_specs=[
            pl.BlockSpec(memory_space=pltpu.SMEM),
            block,
            b_block,
            c_block,
            column,
            row,
            row,
        ],
        out_specs=block,
        out_shape=jax.ShapeDtypeStruct((2 * rows, inner), F32),
        scratch_shapes=[pltpu.VMEM((rows, rows), F32)],
        compiler_params=params(2),
        cost_estimate=pl.CostEstimate(
            flops=8 * rows * rows * inner,
            bytes_accessed=16 * rows * inner,
            transcendentals=2 * heads * rows * rows,
        ),
    )(skip_gain, xs, bc, bc, cum, step_rows, cum_rows)

    normed = pl.pallas_call(
        norm_body,
        grid=grid,
        in_specs=[
            block,
            c_block,
            column,
            block,
            pl.BlockSpec((1, head_dim), lambda b, h: (0, h)),
            pl.BlockSpec((1, 1, nstate, head_dim), lambda b, h: (b, h, 0, 0)),
        ],
        out_specs=pl.BlockSpec((rows, head_dim), lambda b, h: (0, b * heads + h)),
        out_shape=jax.ShapeDtypeStruct((rows, 2 * inner), BF16),
        compiler_params=params(2),
    )(y, bc, cum, gate, norm_gain[None, :], enter)

    summed = output_sum(normed, out_proj, partner, tokens.shape[1])
    return (summed * keep_mask.astype(F32) * (1.0 / 0.9)).astype(BF16)


def solution(mesh):
    return jax.shard_map(
        shards,
        mesh=mesh,
        in_specs=(
            P("seq", "chan"),
            P(None, "chan"),
            P(None, "chan"),
            P(),
            P(None, "chan"),
            P("chan"),
            P("chan"),
            P("chan"),
            P(None, "chan"),
            P("chan"),
            P("chan", None),
            P(),
            P("seq", "chan"),
        ),
        out_specs=P("seq", "chan"),
        check_vma=False,
    )
```

```python
import functools

import jax
import jax.numpy as jnp
from jax import lax
from jax.experimental import pallas as pl
from jax.experimental.pallas import tpu as pltpu
from jax.sharding import PartitionSpec as P

KW = 4
HALO = 16
TILE = 256
DEPTH = 256
MESH = pl.DeviceIdType.MESH
F32 = jnp.float32
BF16 = jnp.bfloat16
VMEM_LIMIT = 50 * 1024 * 1024


def params(grid_rank):
    return pltpu.CompilerParams(
        dimension_semantics=("arbitrary",) * grid_rank, vmem_limit_bytes=VMEM_LIMIT
    )


def chosen_rows(partner, low, depth):
    local = jnp.clip(partner - low, -1, depth).astype(F32).astype(BF16)
    source = lax.broadcasted_iota(jnp.int32, (depth, partner.shape[1]), 0)
    source = source.astype(F32).astype(BF16)
    return jnp.where(source == local, jnp.ones((), BF16), jnp.zeros((), BF16))


def gather_body(tokens_ref, partner_ref, out_ref, send_sem, recv_sem):
    rows, cols = tokens_ref.shape
    width = out_ref.shape[1]
    half = rows // 2
    me = lax.axis_index("chan")
    mate, beside, above = flip(me, 1), flip(me, 2), flip(me, 4)
    opposite = flip(beside, 4)
    greet((mate, beside, above))
    every, low, high = pl.ds(0, rows), pl.ds(0, half), pl.ds(half, half)

    def at(block):
        return pl.ds(pl.multiple_of(block * cols, cols), cols)

    out_ref[:rows, at(me)] = tokens_ref[...]

    def remote(index, part, owner, to):
        piece = out_ref.at[part, at(owner)]
        return pltpu.make_async_remote_copy(
            src_ref=piece, dst_ref=piece,
            send_sem=send_sem.at[index], recv_sem=recv_sem.at[index],
            device_id={"chan": to}, device_id_type=MESH,
        )

    copies = [
        remote(0, every, me, mate),
        remote(1, low, me, beside),
        remote(2, high, me, beside),
        remote(3, high, me, above),
        remote(4, low, me, above),
        remote(5, low, beside, above),
        remote(6, high, above, beside),
        remote(7, every, beside, mate),
        remote(8, every, above, mate),
        remote(9, low, opposite, mate),
        remote(10, high, opposite, mate),
    ]

    def permute(block, initial):
        def tile(column, carry):
            partner = partner_ref[:, at(column)]
            part = jnp.zeros((rows, cols), F32)
            for owner in (block, flip(block, 1)):
                for depth in range(0, cols, DEPTH):
                    start = pl.multiple_of(owner * cols + depth, DEPTH)
                    part += jnp.dot(
                        out_ref[:rows, pl.ds(start, DEPTH)],
                        chosen_rows(partner, start, DEPTH),
                        preferred_element_type=F32,
                    )
            if not initial:
                part += out_ref[rows:, at(column)].astype(F32)
            out_ref[rows:, at(column)] = part.astype(BF16)
            return carry

        lax.fori_loop(0, width // cols, tile, 0)

    for index in (1, 3, 0, 2, 4):
        copies[index].start()
    copies[0].wait_recv()
    permute(me, True)
    for arrived, onward in ((1, 5), (3, 6), (2, 7), (4, 8)):
        copies[arrived].wait_recv()
        copies[onward].start()
    copies[7].wait_recv()
    permute(beside, False)
    for arrived, onward in ((5, 9), (6, 10)):
        copies[arrived].wait_recv()
        copies[onward].start()
    copies[8].wait_recv()
    permute(above, False)
    copies[9].wait_recv()
    copies[10].wait_recv()
    permute(opposite, False)
    for copy in copies:
        copy.wait_send()


def gather_both(tokens, partner):
    rows, width = tokens.shape[0], partner.shape[1]
    vmem = pl.BlockSpec(memory_space=pltpu.VMEM)
    return pl.pallas_call(
        gather_body,
        in_specs=[vmem] * 2,
        out_specs=vmem,
        out_shape=jax.ShapeDtypeStruct((2 * rows, width), BF16),
        scratch_shapes=[pltpu.SemaphoreType.DMA((11,)), pltpu.SemaphoreType.DMA((11,))],
        compiler_params=pltpu.CompilerParams(
            collective_id=3, has_side_effects=True, vmem_limit_bytes=VMEM_LIMIT
        ),
        cost_estimate=pl.CostEstimate(
            flops=2 * rows * width * width, bytes_accessed=6 * rows * width, transcendentals=0
        ),
    )(tokens, partner)


def product_body(counts, a_ref, *refs):
    step = pl.program_id(0)
    begin = 0
    for index, count in enumerate(counts):
        weight_ref, out_ref = refs[index], refs[len(counts) + index]

        @pl.when((step >= begin) & (step < begin + count))
        def _(weight_ref=weight_ref, out_ref=out_ref):
            out_ref[...] = jnp.dot(
                a_ref[...], weight_ref[...], preferred_element_type=F32
            ).astype(BF16)

        begin += count


def products(a, weights):
    rows, depth = a.shape
    counts = tuple(w.shape[1] // TILE for w in weights)
    steps = sum(counts)

    def tile_of(index):
        begin = sum(counts[:index])
        return lambda j: (0, jnp.clip(j - begin, 0, counts[index] - 1))

    return pl.pallas_call(
        functools.partial(product_body, counts),
        grid=(steps,),
        in_specs=[pl.BlockSpec((rows, depth), lambda j: (0, 0))]
        + [pl.BlockSpec((depth, TILE), tile_of(i)) for i in range(len(weights))],
        out_specs=[pl.BlockSpec((rows, TILE), tile_of(i)) for i in range(len(weights))],
        out_shape=[jax.ShapeDtypeStruct((rows, w.shape[1]), BF16) for w in weights],
        compiler_params=params(1),
        cost_estimate=pl.CostEstimate(
            flops=2 * rows * depth * TILE * steps,
            bytes_accessed=2 * (rows * depth + (depth + rows) * TILE * steps),
            transcendentals=0,
        ),
    )(a, *weights)


def silu(v):
    return 0.5 * v * (1.0 + jnp.tanh(0.5 * v))


def column_of(ref, head):
    values = ref[...]
    lanes = lax.broadcasted_iota(jnp.int32, values.shape, 1)
    return jnp.sum(jnp.where(lanes == head, values, 0.0), axis=1, keepdims=True)


def state_body(value_ref, halo_ref, taps_ref, b_ref, step_ref, cum_ref, xs_ref, state_ref):
    branch, head = pl.program_id(0), pl.program_id(1)
    rows = value_ref.shape[0]
    nstate = b_ref.shape[1]
    value = value_ref[...].astype(F32)
    halo = halo_ref[...].astype(F32)
    step = column_of(step_ref, head)
    cum = column_of(cum_ref, head)

    def finish(conv, end):
        xs = silu(conv).astype(BF16)
        xs_ref[...] = xs
        weighted = (xs.astype(F32) * (jnp.exp(end - cum) * step)).astype(BF16)
        state = lax.dot_general(
            b_ref[...], weighted, (((0,), (0,)), ((), ())), preferred_element_type=F32
        )
        state_ref[0, 0, :nstate, :] = state.astype(BF16)
        state_ref[0, 0, nstate:, :] = jnp.broadcast_to(
            jnp.exp(end), (HALO, state.shape[1])
        ).astype(BF16)

    @pl.when(branch == 0)
    def _():
        ext = jnp.concatenate([halo, value], axis=0)
        conv = taps_ref[KW - 1 : KW, :] * value
        for k in range(KW - 1):
            low = HALO - (KW - 1) + k
            conv += taps_ref[k : k + 1, :] * ext[low : low + rows]
        finish(conv, cum[rows - 1 : rows])

    @pl.when(branch == 1)
    def _():
        ext = jnp.concatenate([value, halo], axis=0)
        conv = taps_ref[KW - 1 : KW, :] * value
        for k in range(KW - 1):
            low = KW - 1 - k
            conv += taps_ref[k : k + 1, :] * ext[low : low + rows]
        finish(conv, cum[0:1])


def local_body(skip_ref, xs_ref, b_ref, c_ref, cum_ref, step_row_ref, cum_row_ref, y_ref, scores):
    branch, head = pl.program_id(0), pl.program_id(1)
    rows = xs_ref.shape[0]

    @pl.when(head == 0)
    def _():
        scores[...] = lax.dot_general(
            c_ref[...], b_ref[...], (((1,), (1,)), ((), ())), preferred_element_type=F32
        )

    cum = column_of(cum_ref, head)
    cum_row = cum_row_ref[0]
    step_row = step_row_ref[0]
    xs = xs_ref[...]
    skip = skip_ref[head]
    size = min(TILE, rows)
    below = lax.broadcasted_iota(jnp.int32, (size, size), 0) - lax.broadcasted_iota(
        jnp.int32, (size, size), 1
    )

    def run(sign):
        for t in range(0, rows, size):
            at = slice(t, t + size)
            total = xs[at].astype(F32) * skip
            for s in range(0, rows, size):
                if sign * (t - s) < 0:
                    continue
                gaps = cum[at] - cum_row[:, s : s + size]
                if s == t:
                    gaps = jnp.where(sign * below >= 0, gaps, -jnp.inf)
                mixing = jnp.exp(gaps) * (scores[at, s : s + size] * step_row[:, s : s + size])
                total += jnp.dot(
                    mixing.astype(BF16), xs[s : s + size], preferred_element_type=F32
                )
            y_ref[at, :] = total

    @pl.when(branch == 0)
    def _():
        run(1)

    @pl.when(branch == 1)
    def _():
        run(-1)


def norm_body(y_ref, c_ref, cum_ref, gate_ref, gain_ref, enter_ref, out_ref):
    head = pl.program_id(1)
    cum = column_of(cum_ref, head)
    carried = jnp.dot(c_ref[...], enter_ref[0, 0], preferred_element_type=F32)
    y = y_ref[...] + jnp.exp(cum) * carried
    gate = gate_ref[...].astype(F32)
    gated = y * silu(gate)
    mean = jnp.mean(gated * gated, axis=1, keepdims=True)
    out_ref[...] = (gated * lax.rsqrt(mean + 1e-05) * gain_ref[...]).astype(BF16)


def shift(block, distance):
    count = lax.axis_size("seq")
    route = [(i, i + distance) for i in range(count) if 0 <= i + distance < count]
    return lax.ppermute(block, "seq", route)


def chain_body(packed_ref, enter_ref, inbox, outbox, send_sem, recv_sem):
    heads = packed_ref.shape[1]
    nstate = inbox.shape[2]
    count = lax.axis_size("seq")
    place = lax.axis_index("seq")
    toward = [(place + 1) % count, (place + count - 1) % count]
    first = [place == 0, place == count - 1]
    last = [place == count - 1, place == 0]

    barrier = pltpu.get_barrier_semaphore()
    for branch in (0, 1):

        @pl.when(jnp.logical_not(last[branch]))
        def _(branch=branch):
            pl.semaphore_signal(
                barrier, inc=1, device_id={"seq": toward[branch]}, device_id_type=MESH
            )

    pl.semaphore_wait(barrier, jnp.where(place == 0, 0, 1) + jnp.where(place == count - 1, 0, 1))

    def copy(branch, head):
        return pltpu.make_async_remote_copy(
            src_ref=outbox.at[branch, head],
            dst_ref=inbox.at[branch, head],
            send_sem=send_sem.at[branch, head],
            recv_sem=recv_sem.at[branch, head],
            device_id={"seq": toward[branch]},
            device_id_type=MESH,
        )

    def relay(branch, head):
        copy(branch, head).wait_recv()
        arrived = inbox[branch, head]
        enter_ref[branch, head] = arrived

        @pl.when(jnp.logical_not(last[branch]))
        def _():
            decay = packed_ref[branch, head, nstate : nstate + 1, :].astype(F32)
            end = packed_ref[branch, head, :nstate, :].astype(F32)
            outbox[branch, head] = (decay * arrived.astype(F32) + end).astype(BF16)
            copy(branch, head).start()

    for branch in (0, 1):

        @pl.when(first[branch])
        def _(branch=branch):
            for head in range(heads):
                enter_ref[branch, head] = jnp.zeros(inbox.shape[2:], BF16)
                outbox[branch, head] = packed_ref[branch, head, :nstate, :]
                copy(branch, head).start()

    for near, order in ((2 * place < count, (0, 1)), (2 * place >= count, (1, 0))):
        for branch in order:

            @pl.when(near & jnp.logical_not(first[branch]))
            def _(branch=branch):
                for head in range(heads):
                    relay(branch, head)

    for branch in (0, 1):

        @pl.when(jnp.logical_not(last[branch]))
        def _(branch=branch):
            for head in range(heads):
                copy(branch, head).wait_send()


def entering(packed, nstate):
    _, heads, _, head_dim = packed.shape
    shape = (2, heads, nstate, head_dim)
    vmem = pl.BlockSpec(memory_space=pltpu.VMEM)
    return pl.pallas_call(
        chain_body,
        in_specs=[vmem],
        out_specs=vmem,
        out_shape=jax.ShapeDtypeStruct(shape, BF16),
        scratch_shapes=[
            pltpu.VMEM(shape, BF16),
            pltpu.VMEM(shape, BF16),
            pltpu.SemaphoreType.DMA((2, heads)),
            pltpu.SemaphoreType.DMA((2, heads)),
        ],
        compiler_params=pltpu.CompilerParams(
            collective_id=1, has_side_effects=True, vmem_limit_bytes=VMEM_LIMIT
        ),
    )(packed)


def flip(me, bit):
    return me + bit * (1 - 2 * ((me // bit) % 2))


def greet(partners):
    barrier = pltpu.get_barrier_semaphore()
    for partner in partners:
        pl.semaphore_signal(barrier, inc=1, device_id={"chan": partner}, device_id_type=MESH)
    pl.semaphore_wait(barrier, len(partners))


def output_body(
    normed_ref, table_ref, partner_ref, out_ref,
    reverse, total, mine, theirs, sent, diagonal, across,
    core_send, core_recv, chip_send, chip_recv,
):
    rows, width = reverse.shape
    inner = table_ref.shape[0]
    cols = out_ref.shape[1]
    half = rows // 2
    me = lax.axis_index("chan")
    mate, beside, above = flip(me, 1), flip(me, 2), flip(me, 4)
    greet((mate, beside, above))

    def at(block):
        return pl.ds(pl.multiple_of(block * cols, cols), cols)

    def project(block, carry):
        reverse[:, at(block)] = jnp.dot(
            normed_ref[:, inner:], table_ref[:, at(block)], preferred_element_type=F32
        ).astype(BF16)
        return carry

    lax.fori_loop(0, width // cols, project, 0)

    def remote(src, dst, send_sem, recv_sem, to):
        return pltpu.make_async_remote_copy(
            src_ref=src, dst_ref=dst, send_sem=send_sem, recv_sem=recv_sem,
            device_id={"chan": to}, device_id_type=MESH,
        )

    def core_copy(slot):
        return remote(
            mine.at[slot], theirs.at[slot], core_send.at[slot], core_recv.at[slot], mate
        )

    low, high = pl.ds(0, half), pl.ds(half, half)
    chip_copies = [
        remote(sent.at[0, low], diagonal.at[0], chip_send.at[0], chip_recv.at[0], beside),
        remote(sent.at[0, high], diagonal.at[1], chip_send.at[1], chip_recv.at[1], above),
        remote(sent.at[1, low], across.at[0, low], chip_send.at[2], chip_recv.at[2], beside),
        remote(sent.at[1, high], across.at[0, high], chip_send.at[3], chip_recv.at[3], beside),
        remote(sent.at[2, high], across.at[1, high], chip_send.at[4], chip_recv.at[4], above),
        remote(sent.at[2, low], across.at[1, low], chip_send.at[5], chip_recv.at[5], above),
    ]

    def stage(chip, carry):
        is_beside = (chip == 0) | (chip == 1)
        is_above = (chip == 0) | (chip == 2)
        base = jnp.where(is_beside, beside - me, 0) + jnp.where(is_above, above - me, 0) + me

        def compute(turn, inner_carry):
            block = jnp.where(turn == 0, flip(base, 1), base)
            partner = partner_ref[:, at(block)]
            part = jnp.dot(
                normed_ref[:, :inner], table_ref[:, at(block)], preferred_element_type=F32
            )
            for depth in range(0, width, DEPTH):
                part += jnp.dot(
                    reverse[:, depth : depth + DEPTH],
                    chosen_rows(partner, depth, DEPTH),
                    preferred_element_type=F32,
                )
            total[...] = part

            @pl.when(turn == 0)
            def _():
                mine[chip] = part.astype(BF16)
                core_copy(chip).start()

            return inner_carry

        lax.fori_loop(0, 2, compute, 0)
        core_copy(chip).wait_recv()
        total[...] += theirs[chip].astype(F32)

        @pl.when(chip == 0)
        def _():
            sent[0] = total[...].astype(BF16)
            chip_copies[0].start()
            chip_copies[1].start()

        @pl.when(chip == 1)
        def _():
            sent[1, :half] = total[:half].astype(BF16)
            chip_copies[2].start()
            chip_copies[1].wait_recv()
            sent[1, half:] = (total[half:] + diagonal[1].astype(F32)).astype(BF16)
            chip_copies[3].start()

        @pl.when(chip == 2)
        def _():
            sent[2, half:] = total[half:].astype(BF16)
            chip_copies[4].start()
            chip_copies[0].wait_recv()
            sent[2, :half] = (total[:half] + diagonal[0].astype(F32)).astype(BF16)
            chip_copies[5].start()

        return carry

    lax.fori_loop(0, 4, stage, 0)
    for copy in chip_copies[2:]:
        copy.wait_recv()
    out_ref[...] = total[...] + across[0].astype(F32) + across[1].astype(F32)
    for slot in range(4):
        core_copy(slot).wait_send()
    for copy in chip_copies:
        copy.wait_send()


def output_sum(normed, table, partner, cols):
    rows = normed.shape[0]
    width = table.shape[1]
    vmem = pl.BlockSpec(memory_space=pltpu.VMEM)
    block = (rows, cols)
    return pl.pallas_call(
        output_body,
        in_specs=[vmem] * 3,
        out_specs=vmem,
        out_shape=jax.ShapeDtypeStruct(block, F32),
        scratch_shapes=[
            pltpu.VMEM((rows, width), BF16),
            pltpu.VMEM(block, F32),
            pltpu.VMEM((4,) + block, BF16),
            pltpu.VMEM((4,) + block, BF16),
            pltpu.VMEM((3,) + block, BF16),
            pltpu.VMEM((2, rows // 2, cols), BF16),
            pltpu.VMEM((2,) + block, BF16),
            pltpu.SemaphoreType.DMA((4,)),
            pltpu.SemaphoreType.DMA((4,)),
            pltpu.SemaphoreType.DMA((6,)),
            pltpu.SemaphoreType.DMA((6,)),
        ],
        compiler_params=pltpu.CompilerParams(
            collective_id=2, has_side_effects=True, vmem_limit_bytes=VMEM_LIMIT
        ),
        cost_estimate=pl.CostEstimate(
            flops=2 * rows * width * (2 * table.shape[0] + width),
            bytes_accessed=2 * table.size + 2 * normed.size,
            transcendentals=0,
        ),
    )(normed, table, partner)


def shards(
    tokens,
    gate_proj,
    value_proj,
    state_proj,
    step_proj,
    step_bias,
    decay_rate,
    skip_gain,
    conv_kernel,
    norm_gain,
    out_proj,
    complement,
    keep_mask,
):
    rows = tokens.shape[0]
    inner = gate_proj.shape[1]
    heads = step_proj.shape[1]
    head_dim = inner // heads
    nstate = state_proj.shape[1] // 2
    partner = complement[None, :]

    both = gather_both(tokens, partner)
    value, bc = products(both, (value_proj, state_proj))
    halo = jnp.concatenate(
        [shift(value[rows - HALO : rows], 1), shift(value[rows : rows + HALO], -1)], axis=0
    )
    step_raw = jnp.dot(both, step_proj, preferred_element_type=F32)
    step = jax.nn.softplus(step_raw + step_bias).reshape(2, rows, heads)
    log_decay = -step * decay_rate
    cum = jnp.stack(
        [jnp.cumsum(log_decay[0], axis=0), lax.cumsum(log_decay[1], axis=0, reverse=True)]
    )
    step_rows = jnp.swapaxes(step, 1, 2).reshape(2 * heads, 1, rows)
    cum_rows = jnp.swapaxes(cum, 1, 2).reshape(2 * heads, 1, rows)
    step = step.reshape(2 * rows, heads)
    cum = cum.reshape(2 * rows, heads)
    (gate,) = products(both, (gate_proj,))

    grid = (2, heads)
    block = pl.BlockSpec((rows, head_dim), lambda b, h: (b, h))
    b_block = pl.BlockSpec((rows, nstate), lambda b, h: (b, 0))
    c_block = pl.BlockSpec((rows, nstate), lambda b, h: (b, 1))
    column = pl.BlockSpec((rows, heads), lambda b, h: (b, 0))
    row = pl.BlockSpec((1, 1, rows), lambda b, h: (b * heads + h, 0, 0))

    xs, packed = pl.pallas_call(
        state_body,
        grid=grid,
        in_specs=[
            block,
            pl.BlockSpec((HALO, head_dim), lambda b, h: (b, h)),
            pl.BlockSpec((KW, head_dim), lambda b, h: (0, h)),
            b_block,
            column,
            column,
        ],
        out_specs=[
            block,
            pl.BlockSpec((1, 1, nstate + HALO, head_dim), lambda b, h: (b, h, 0, 0)),
        ],
        out_shape=[
            jax.ShapeDtypeStruct((2 * rows, inner), BF16),
            jax.ShapeDtypeStruct((2, heads, nstate + HALO, head_dim), BF16),
        ],
        compiler_params=params(2),
    )(value, halo, conv_kernel, bc, step, cum)

    enter = entering(packed, nstate)

    y = pl.pallas_call(
        local_body,
        grid=grid,
        in_specs=[
            pl.BlockSpec(memory_space=pltpu.SMEM),
            block,
            b_block,
            c_block,
            column,
            row,
            row,
        ],
        out_specs=block,
        out_shape=jax.ShapeDtypeStruct((2 * rows, inner), F32),
        scratch_shapes=[pltpu.VMEM((rows, rows), F32)],
        compiler_params=params(2),
        cost_estimate=pl.CostEstimate(
            flops=8 * rows * rows * inner,
            bytes_accessed=16 * rows * inner,
            transcendentals=2 * heads * rows * rows,
        ),
    )(skip_gain, xs, bc, bc, cum, step_rows, cum_rows)

    normed = pl.pallas_call(
        norm_body,
        grid=grid,
        in_specs=[
            block,
            c_block,
            column,
            block,
            pl.BlockSpec((1, head_dim), lambda b, h: (0, h)),
            pl.BlockSpec((1, 1, nstate, head_dim), lambda b, h: (b, h, 0, 0)),
        ],
        out_specs=pl.BlockSpec((rows, head_dim), lambda b, h: (0, b * heads + h)),
        out_shape=jax.ShapeDtypeStruct((rows, 2 * inner), BF16),
        compiler_params=params(2),
    )(y, bc, cum, gate, norm_gain[None, :], enter)

    summed = output_sum(normed, out_proj, partner, tokens.shape[1])
    return (summed * keep_mask.astype(F32) * (1.0 / 0.9)).astype(BF16)


def solution(mesh):
    return jax.shard_map(
        shards,
        mesh=mesh,
        in_specs=(
            P("seq", "chan"),
            P(None, "chan"),
            P(None, "chan"),
            P(),
            P(None, "chan"),
            P("chan"),
            P("chan"),
            P("chan"),
            P(None, "chan"),
            P("chan"),
            P("chan", None),
            P(),
            P("seq", "chan"),
        ),
        out_specs=P("seq", "chan"),
        check_vma=False,
    )
```

```python
import functools

import jax
import jax.numpy as jnp
from jax import lax
from jax.experimental import pallas as pl
from jax.experimental.pallas import tpu as pltpu
from jax.sharding import PartitionSpec as P

KW = 4
HALO = 16
TILE = 256
DEPTH = 256
MESH = pl.DeviceIdType.MESH
F32 = jnp.float32
BF16 = jnp.bfloat16
VMEM_LIMIT = 50 * 1024 * 1024


def params(grid_rank):
    return pltpu.CompilerParams(
        dimension_semantics=("arbitrary",) * grid_rank, vmem_limit_bytes=VMEM_LIMIT
    )


def chosen_rows(partner, low, depth):
    local = jnp.clip(partner - low, -1, depth).astype(F32).astype(BF16)
    source = lax.broadcasted_iota(jnp.int32, (depth, partner.shape[1]), 0)
    source = source.astype(F32).astype(BF16)
    return jnp.where(source == local, jnp.ones((), BF16), jnp.zeros((), BF16))


def gather_body(tokens_ref, partner_ref, out_ref, send_sem, recv_sem):
    rows, cols = tokens_ref.shape
    width = out_ref.shape[1]
    half = rows // 2
    me = lax.axis_index("chan")
    mate, beside, above = flip(me, 1), flip(me, 2), flip(me, 4)
    opposite = flip(beside, 4)
    greet((mate, beside, above))
    every, low, high = pl.ds(0, rows), pl.ds(0, half), pl.ds(half, half)

    def at(block):
        return pl.ds(pl.multiple_of(block * cols, cols), cols)

    out_ref[:rows, at(me)] = tokens_ref[...]

    def remote(index, part, owner, to):
        piece = out_ref.at[part, at(owner)]
        return pltpu.make_async_remote_copy(
            src_ref=piece, dst_ref=piece,
            send_sem=send_sem.at[index], recv_sem=recv_sem.at[index],
            device_id={"chan": to}, device_id_type=MESH,
        )

    copies = [
        remote(0, every, me, mate),
        remote(1, low, me, beside),
        remote(2, high, me, beside),
        remote(3, high, me, above),
        remote(4, low, me, above),
        remote(5, low, beside, above),
        remote(6, high, above, beside),
        remote(7, every, beside, mate),
        remote(8, every, above, mate),
        remote(9, low, opposite, mate),
        remote(10, high, opposite, mate),
    ]

    def permute(block, initial):
        def tile(column, carry):
            partner = partner_ref[:, at(column)]
            part = jnp.zeros((rows, cols), F32)
            for owner in (block, flip(block, 1)):
                for depth in range(0, cols, DEPTH):
                    start = pl.multiple_of(owner * cols + depth, DEPTH)
                    part += jnp.dot(
                        out_ref[:rows, pl.ds(start, DEPTH)],
                        chosen_rows(partner, start, DEPTH),
                        preferred_element_type=F32,
                    )
            if not initial:
                part += out_ref[rows:, at(column)].astype(F32)
            out_ref[rows:, at(column)] = part.astype(BF16)
            return carry

        lax.fori_loop(0, width // cols, tile, 0)

    for index in (1, 3, 0, 2, 4):
        copies[index].start()
    copies[0].wait_recv()
    permute(me, True)
    for arrived, onward in ((1, 5), (3, 6), (2, 7), (4, 8)):
        copies[arrived].wait_recv()
        copies[onward].start()
    copies[7].wait_recv()
    permute(beside, False)
    for arrived, onward in ((5, 9), (6, 10)):
        copies[arrived].wait_recv()
        copies[onward].start()
    copies[8].wait_recv()
    permute(above, False)
    copies[9].wait_recv()
    copies[10].wait_recv()
    permute(opposite, False)
    for copy in copies:
        copy.wait_send()


def gather_both(tokens, partner):
    rows, width = tokens.shape[0], partner.shape[1]
    vmem = pl.BlockSpec(memory_space=pltpu.VMEM)
    return pl.pallas_call(
        gather_body,
        in_specs=[vmem] * 2,
        out_specs=vmem,
        out_shape=jax.ShapeDtypeStruct((2 * rows, width), BF16),
        scratch_shapes=[pltpu.SemaphoreType.DMA((11,)), pltpu.SemaphoreType.DMA((11,))],
        compiler_params=pltpu.CompilerParams(
            collective_id=3, has_side_effects=True, vmem_limit_bytes=VMEM_LIMIT
        ),
        cost_estimate=pl.CostEstimate(
            flops=2 * rows * width * width, bytes_accessed=6 * rows * width, transcendentals=0
        ),
    )(tokens, partner)


def product_body(counts, a_ref, *refs):
    step = pl.program_id(0)
    begin = 0
    for index, count in enumerate(counts):
        weight_ref, out_ref = refs[index], refs[len(counts) + index]

        @pl.when((step >= begin) & (step < begin + count))
        def _(weight_ref=weight_ref, out_ref=out_ref):
            out_ref[...] = jnp.dot(
                a_ref[...], weight_ref[...], preferred_element_type=F32
            ).astype(BF16)

        begin += count


def products(a, weights):
    rows, depth = a.shape
    counts = tuple(w.shape[1] // TILE for w in weights)
    steps = sum(counts)

    def tile_of(index):
        begin = sum(counts[:index])
        return lambda j: (0, jnp.clip(j - begin, 0, counts[index] - 1))

    return pl.pallas_call(
        functools.partial(product_body, counts),
        grid=(steps,),
        in_specs=[pl.BlockSpec((rows, depth), lambda j: (0, 0))]
        + [pl.BlockSpec((depth, TILE), tile_of(i)) for i in range(len(weights))],
        out_specs=[pl.BlockSpec((rows, TILE), tile_of(i)) for i in range(len(weights))],
        out_shape=[jax.ShapeDtypeStruct((rows, w.shape[1]), BF16) for w in weights],
        compiler_params=params(1),
        cost_estimate=pl.CostEstimate(
            flops=2 * rows * depth * TILE * steps,
            bytes_accessed=2 * (rows * depth + (depth + rows) * TILE * steps),
            transcendentals=0,
        ),
    )(a, *weights)


def silu(v):
    return 0.5 * v * (1.0 + jnp.tanh(0.5 * v))


def column_of(values, head):
    lanes = lax.broadcasted_iota(jnp.int32, values.shape, 1)
    return jnp.sum(jnp.where(lanes == head, values, 0.0), axis=1, keepdims=True)


def state_body(value_ref, halo_ref, taps_ref, b_ref, step_ref, cum_ref, xs_ref, state_ref):
    branch, head = pl.program_id(0), pl.program_id(1)
    rows = value_ref.shape[0]
    nstate = b_ref.shape[1]
    value = value_ref[...].astype(F32)
    halo = halo_ref[...].astype(F32)
    step = column_of(step_ref[...], head)
    cum = column_of(cum_ref[...], head)

    def finish(conv, end):
        xs = silu(conv).astype(BF16)
        xs_ref[...] = xs
        weighted = (xs.astype(F32) * (jnp.exp(end - cum) * step)).astype(BF16)
        state = lax.dot_general(
            b_ref[...], weighted, (((0,), (0,)), ((), ())), preferred_element_type=F32
        )
        state_ref[0, 0, :nstate, :] = state.astype(BF16)
        state_ref[0, 0, nstate:, :] = jnp.broadcast_to(
            jnp.exp(end), (HALO, state.shape[1])
        ).astype(BF16)

    @pl.when(branch == 0)
    def _():
        ext = jnp.concatenate([halo, value], axis=0)
        conv = taps_ref[KW - 1 : KW, :] * value
        for k in range(KW - 1):
            low = HALO - (KW - 1) + k
            conv += taps_ref[k : k + 1, :] * ext[low : low + rows]
        finish(conv, cum[rows - 1 : rows])

    @pl.when(branch == 1)
    def _():
        ext = jnp.concatenate([value, halo], axis=0)
        conv = taps_ref[KW - 1 : KW, :] * value
        for k in range(KW - 1):
            low = KW - 1 - k
            conv += taps_ref[k : k + 1, :] * ext[low : low + rows]
        finish(conv, cum[0:1])


def step_body(raw_ref, bias_ref, rate_ref, step_ref, cum_ref):
    rows = raw_ref.shape[0] // 2
    order = lax.broadcasted_iota(jnp.int32, (rows, rows), 0) - lax.broadcasted_iota(
        jnp.int32, (rows, rows), 1
    )
    for branch in (0, 1):
        part = pl.ds(branch * rows, rows)
        raw = raw_ref[part, :] + bias_ref[...]
        step = jnp.maximum(raw, 0.0) + jnp.log1p(jnp.exp(-jnp.abs(raw)))
        summed = jnp.where(order >= 0 if branch == 0 else order <= 0, 1.0, 0.0)
        step_ref[part, :] = step
        cum_ref[part, :] = jnp.dot(
            summed,
            -step * rate_ref[...],
            precision=lax.Precision.HIGHEST,
            preferred_element_type=F32,
        )


def scan_body(
    skip_ref, packed_ref, xs_ref, bc_ref, cum_ref, step_row_ref, cum_row_ref, gate_ref, gain_ref,
    out_ref, scores, local, inbox, outbox, send_sem, recv_sem,
):
    heads = packed_ref.shape[1]
    nstate, head_dim = inbox.shape[2:]
    rows = out_ref.shape[0]
    size = min(TILE, rows)
    count = lax.axis_size("seq")
    place = lax.axis_index("seq")
    toward = [(place + 1) % count, (place + count - 1) % count]
    first = [place == 0, place == count - 1]
    last = [place == count - 1, place == 0]

    barrier = pltpu.get_barrier_semaphore()
    for branch in (0, 1):

        @pl.when(jnp.logical_not(last[branch]))
        def _(branch=branch):
            pl.semaphore_signal(
                barrier, inc=1, device_id={"seq": toward[branch]}, device_id_type=MESH
            )

    pl.semaphore_wait(barrier, jnp.where(place == 0, 0, 1) + jnp.where(place == count - 1, 0, 1))

    def copy(branch, head):
        return pltpu.make_async_remote_copy(
            src_ref=outbox.at[branch, head],
            dst_ref=inbox.at[branch, head],
            send_sem=send_sem.at[branch, head],
            recv_sem=recv_sem.at[branch, head],
            device_id={"seq": toward[branch]},
            device_id_type=MESH,
        )

    def relay(branch, head):
        copy(branch, head).wait_recv()

        @pl.when(jnp.logical_not(last[branch]))
        def _():
            decay = packed_ref[branch, head, nstate : nstate + 1, :].astype(F32)
            end = packed_ref[branch, head, :nstate, :].astype(F32)
            arrived = inbox[branch, head].astype(F32)
            outbox[branch, head] = (decay * arrived + end).astype(BF16)
            copy(branch, head).start()

    def lanes(head):
        return pl.ds(pl.multiple_of(head * head_dim, head_dim), head_dim)

    def within(branch):
        base = branch * rows
        part = pl.ds(base, rows)
        scores[...] = lax.dot_general(
            bc_ref[part, nstate:],
            bc_ref[part, :nstate],
            (((1,), (1,)), ((), ())),
            preferred_element_type=F32,
        )
        sign = 1 - 2 * branch
        below = lax.broadcasted_iota(jnp.int32, (size, size), 0) - lax.broadcasted_iota(
            jnp.int32, (size, size), 1
        )

        def one(head, carry):
            cum = column_of(cum_ref[part, :], head)
            cum_row = cum_row_ref[branch * heads + head]
            step_row = step_row_ref[branch * heads + head]
            skip = skip_ref[head]
            xs = xs_ref[part, lanes(head)]
            for t in range(0, rows, size):
                at = slice(t, t + size)
                total = xs[at].astype(F32) * skip
                for s in range(0, rows, size):
                    if sign * (t - s) < 0:
                        continue
                    gaps = cum[at] - cum_row[:, s : s + size]
                    if s == t:
                        gaps = jnp.where(sign * below >= 0, gaps, -jnp.inf)
                    mixing = jnp.exp(gaps) * (scores[at, s : s + size] * step_row[:, s : s + size])
                    total += jnp.dot(
                        mixing.astype(BF16), xs[s : s + size], preferred_element_type=F32
                    )
                local[base + t : base + t + size, lanes(head)] = total
            return carry

        lax.fori_loop(0, heads, one, 0)

    def normalize(branch):
        part = pl.ds(branch * rows, rows)

        def one(head, carry):
            cum = column_of(cum_ref[part, :], head)
            carried = jnp.dot(
                bc_ref[part, nstate:], inbox[branch, head], preferred_element_type=F32
            )
            y = local[part, lanes(head)] + jnp.exp(cum) * carried
            gated = y * silu(gate_ref[part, lanes(head)].astype(F32))
            mean = jnp.mean(gated * gated, axis=1, keepdims=True)
            normed = gated * lax.rsqrt(mean + 1e-05) * gain_ref[:, lanes(head)]
            out_ref[:, lanes(branch * heads + head)] = normed.astype(BF16)
            return carry

        lax.fori_loop(0, heads, one, 0)

    for branch in (0, 1):

        @pl.when(first[branch])
        def _(branch=branch):
            for head in range(heads):
                inbox[branch, head] = jnp.zeros(inbox.shape[2:], BF16)
                outbox[branch, head] = packed_ref[branch, head, :nstate, :]
                copy(branch, head).start()

    def relays(near, branch):
        @pl.when(near & jnp.logical_not(first[branch]))
        def _():
            for head in range(heads):
                relay(branch, head)

    forward_near, reverse_near = 2 * place < count, 2 * place >= count
    relays(forward_near, 0)
    relays(reverse_near, 1)
    within(0)
    relays(forward_near, 1)
    relays(reverse_near, 0)
    within(1)
    normalize(0)
    normalize(1)

    for branch in (0, 1):

        @pl.when(jnp.logical_not(last[branch]))
        def _(branch=branch):
            for head in range(heads):
                copy(branch, head).wait_send()


def shift(block, distance):
    count = lax.axis_size("seq")
    route = [(i, i + distance) for i in range(count) if 0 <= i + distance < count]
    return lax.ppermute(block, "seq", route)


def flip(me, bit):
    return me + bit * (1 - 2 * ((me // bit) % 2))


def greet(partners):
    barrier = pltpu.get_barrier_semaphore()
    for partner in partners:
        pl.semaphore_signal(barrier, inc=1, device_id={"chan": partner}, device_id_type=MESH)
    pl.semaphore_wait(barrier, len(partners))


def output_body(
    normed_ref, table_ref, partner_ref, out_ref,
    reverse, total, mine, theirs, sent, diagonal, across,
    core_send, core_recv, chip_send, chip_recv,
):
    rows, width = reverse.shape
    inner = table_ref.shape[0]
    cols = out_ref.shape[1]
    half = rows // 2
    me = lax.axis_index("chan")
    mate, beside, above = flip(me, 1), flip(me, 2), flip(me, 4)
    greet((mate, beside, above))

    def at(block):
        return pl.ds(pl.multiple_of(block * cols, cols), cols)

    def project(block, carry):
        reverse[:, at(block)] = jnp.dot(
            normed_ref[:, inner:], table_ref[:, at(block)], preferred_element_type=F32
        ).astype(BF16)
        return carry

    lax.fori_loop(0, width // cols, project, 0)

    def remote(src, dst, send_sem, recv_sem, to):
        return pltpu.make_async_remote_copy(
            src_ref=src, dst_ref=dst, send_sem=send_sem, recv_sem=recv_sem,
            device_id={"chan": to}, device_id_type=MESH,
        )

    def core_copy(slot):
        return remote(
            mine.at[slot], theirs.at[slot], core_send.at[slot], core_recv.at[slot], mate
        )

    low, high = pl.ds(0, half), pl.ds(half, half)
    chip_copies = [
        remote(sent.at[0, low], diagonal.at[0], chip_send.at[0], chip_recv.at[0], beside),
        remote(sent.at[0, high], diagonal.at[1], chip_send.at[1], chip_recv.at[1], above),
        remote(sent.at[1, low], across.at[0, low], chip_send.at[2], chip_recv.at[2], beside),
        remote(sent.at[1, high], across.at[0, high], chip_send.at[3], chip_recv.at[3], beside),
        remote(sent.at[2, high], across.at[1, high], chip_send.at[4], chip_recv.at[4], above),
        remote(sent.at[2, low], across.at[1, low], chip_send.at[5], chip_recv.at[5], above),
    ]

    def stage(chip, carry):
        is_beside = (chip == 0) | (chip == 1)
        is_above = (chip == 0) | (chip == 2)
        base = jnp.where(is_beside, beside - me, 0) + jnp.where(is_above, above - me, 0) + me

        def compute(turn, inner_carry):
            block = jnp.where(turn == 0, flip(base, 1), base)
            partner = partner_ref[:, at(block)]
            part = jnp.dot(
                normed_ref[:, :inner], table_ref[:, at(block)], preferred_element_type=F32
            )
            for depth in range(0, width, DEPTH):
                part += jnp.dot(
                    reverse[:, depth : depth + DEPTH],
                    chosen_rows(partner, depth, DEPTH),
                    preferred_element_type=F32,
                )
            total[...] = part

            @pl.when(turn == 0)
            def _():
                mine[chip] = part.astype(BF16)
                core_copy(chip).start()

            return inner_carry

        lax.fori_loop(0, 2, compute, 0)
        core_copy(chip).wait_recv()
        total[...] += theirs[chip].astype(F32)

        @pl.when(chip == 0)
        def _():
            sent[0] = total[...].astype(BF16)
            chip_copies[0].start()
            chip_copies[1].start()

        @pl.when(chip == 1)
        def _():
            sent[1, :half] = total[:half].astype(BF16)
            chip_copies[2].start()
            chip_copies[1].wait_recv()
            sent[1, half:] = (total[half:] + diagonal[1].astype(F32)).astype(BF16)
            chip_copies[3].start()

        @pl.when(chip == 2)
        def _():
            sent[2, half:] = total[half:].astype(BF16)
            chip_copies[4].start()
            chip_copies[0].wait_recv()
            sent[2, :half] = (total[:half] + diagonal[0].astype(F32)).astype(BF16)
            chip_copies[5].start()

        return carry

    lax.fori_loop(0, 4, stage, 0)
    for copy in chip_copies[2:]:
        copy.wait_recv()
    out_ref[...] = total[...] + across[0].astype(F32) + across[1].astype(F32)
    for slot in range(4):
        core_copy(slot).wait_send()
    for copy in chip_copies:
        copy.wait_send()


def output_sum(normed, table, partner, cols):
    rows = normed.shape[0]
    width = table.shape[1]
    vmem = pl.BlockSpec(memory_space=pltpu.VMEM)
    block = (rows, cols)
    return pl.pallas_call(
        output_body,
        in_specs=[vmem] * 3,
        out_specs=vmem,
        out_shape=jax.ShapeDtypeStruct(block, F32),
        scratch_shapes=[
            pltpu.VMEM((rows, width), BF16),
            pltpu.VMEM(block, F32),
            pltpu.VMEM((4,) + block, BF16),
            pltpu.VMEM((4,) + block, BF16),
            pltpu.VMEM((3,) + block, BF16),
            pltpu.VMEM((2, rows // 2, cols), BF16),
            pltpu.VMEM((2,) + block, BF16),
            pltpu.SemaphoreType.DMA((4,)),
            pltpu.SemaphoreType.DMA((4,)),
            pltpu.SemaphoreType.DMA((6,)),
            pltpu.SemaphoreType.DMA((6,)),
        ],
        compiler_params=pltpu.CompilerParams(
            collective_id=2, has_side_effects=True, vmem_limit_bytes=VMEM_LIMIT
        ),
        cost_estimate=pl.CostEstimate(
            flops=2 * rows * width * (2 * table.shape[0] + width),
            bytes_accessed=2 * table.size + 2 * normed.size,
            transcendentals=0,
        ),
    )(normed, table, partner)


def shards(
    tokens,
    gate_proj,
    value_proj,
    state_proj,
    step_proj,
    step_bias,
    decay_rate,
    skip_gain,
    conv_kernel,
    norm_gain,
    out_proj,
    complement,
    keep_mask,
):
    rows = tokens.shape[0]
    inner = gate_proj.shape[1]
    heads = step_proj.shape[1]
    head_dim = inner // heads
    nstate = state_proj.shape[1] // 2
    partner = complement[None, :]

    both = gather_both(tokens, partner)
    value, bc = products(both, (value_proj, state_proj))
    halo = jnp.concatenate(
        [shift(value[rows - HALO : rows], 1), shift(value[rows : rows + HALO], -1)], axis=0
    )
    step_raw = jnp.dot(both, step_proj, preferred_element_type=F32)
    per_step = jax.ShapeDtypeStruct((2 * rows, heads), F32)
    step, cum = pl.pallas_call(
        step_body, out_shape=[per_step, per_step], compiler_params=params(0)
    )(step_raw, step_bias[None, :], decay_rate[None, :])

    def as_rows(a):
        return jnp.swapaxes(a.reshape(2, rows, heads), 1, 2).reshape(2 * heads, 1, rows)

    step_rows, cum_rows = as_rows(step), as_rows(cum)
    (gate,) = products(both, (gate_proj,))

    grid = (2, heads)
    block = pl.BlockSpec((rows, head_dim), lambda b, h: (b, h))
    b_block = pl.BlockSpec((rows, nstate), lambda b, h: (b, 0))
    column = pl.BlockSpec((rows, heads), lambda b, h: (b, 0))

    xs, packed = pl.pallas_call(
        state_body,
        grid=grid,
        in_specs=[
            block,
            pl.BlockSpec((HALO, head_dim), lambda b, h: (b, h)),
            pl.BlockSpec((KW, head_dim), lambda b, h: (0, h)),
            b_block,
            column,
            column,
        ],
        out_specs=[
            block,
            pl.BlockSpec((1, 1, nstate + HALO, head_dim), lambda b, h: (b, h, 0, 0)),
        ],
        out_shape=[
            jax.ShapeDtypeStruct((2 * rows, inner), BF16),
            jax.ShapeDtypeStruct((2, heads, nstate + HALO, head_dim), BF16),
        ],
        compiler_params=params(2),
    )(value, halo, conv_kernel, bc, step, cum)

    vmem = pl.BlockSpec(memory_space=pltpu.VMEM)
    states = (2, heads, nstate, head_dim)
    normed = pl.pallas_call(
        scan_body,
        in_specs=[pl.BlockSpec(memory_space=pltpu.SMEM)] + [vmem] * 8,
        out_specs=vmem,
        out_shape=jax.ShapeDtypeStruct((rows, 2 * inner), BF16),
        scratch_shapes=[
            pltpu.VMEM((rows, rows), F32),
            pltpu.VMEM((2 * rows, inner), F32),
            pltpu.VMEM(states, BF16),
            pltpu.VMEM(states, BF16),
            pltpu.SemaphoreType.DMA((2, heads)),
            pltpu.SemaphoreType.DMA((2, heads)),
        ],
        compiler_params=pltpu.CompilerParams(
            collective_id=1, has_side_effects=True, vmem_limit_bytes=VMEM_LIMIT
        ),
        cost_estimate=pl.CostEstimate(
            flops=8 * rows * rows * inner,
            bytes_accessed=16 * rows * inner,
            transcendentals=2 * heads * rows * rows,
        ),
    )(skip_gain, packed, xs, bc, cum, step_rows, cum_rows, gate, norm_gain[None, :])

    summed = output_sum(normed, out_proj, partner, tokens.shape[1])
    return (summed * keep_mask.astype(F32) * (1.0 / 0.9)).astype(BF16)


def solution(mesh):
    return jax.shard_map(
        shards,
        mesh=mesh,
        in_specs=(
            P("seq", "chan"),
            P(None, "chan"),
            P(None, "chan"),
            P(),
            P(None, "chan"),
            P("chan"),
            P("chan"),
            P("chan"),
            P(None, "chan"),
            P("chan"),
            P("chan", None),
            P(),
            P("seq", "chan"),
        ),
        out_specs=P("seq", "chan"),
        check_vma=False,
    )
```

```python
import functools

import jax
import jax.numpy as jnp
from jax import lax
from jax.experimental import pallas as pl
from jax.experimental.pallas import tpu as pltpu
from jax.sharding import PartitionSpec as P

KW = 4
HALO = 16
TILE = 256
DEPTH = 256
MESH = pl.DeviceIdType.MESH
F32 = jnp.float32
BF16 = jnp.bfloat16
VMEM_LIMIT = 50 * 1024 * 1024


def params(grid_rank):
    return pltpu.CompilerParams(
        dimension_semantics=("arbitrary",) * grid_rank, vmem_limit_bytes=VMEM_LIMIT
    )


def chosen_rows(partner, low, depth):
    local = jnp.clip(partner - low, -1, depth).astype(F32).astype(BF16)
    source = lax.broadcasted_iota(jnp.int32, (depth, partner.shape[1]), 0)
    source = source.astype(F32).astype(BF16)
    return jnp.where(source == local, jnp.ones((), BF16), jnp.zeros((), BF16))


def chosen_deep(partner, low, depth):
    return jnp.concatenate(
        [chosen_rows(partner, low + part, DEPTH) for part in range(0, depth, DEPTH)], axis=0
    )


def gather_body(tokens_ref, partner_ref, out_ref, send_sem, recv_sem):
    rows, cols = tokens_ref.shape
    width = out_ref.shape[1]
    half = rows // 2
    me = lax.axis_index("chan")
    mate, beside, above = flip(me, 1), flip(me, 2), flip(me, 4)
    opposite = flip(beside, 4)
    greet((mate, beside, above))
    every, low, high = pl.ds(0, rows), pl.ds(0, half), pl.ds(half, half)

    def at(block):
        return pl.ds(pl.multiple_of(block * cols, cols), cols)

    out_ref[:rows, at(me)] = tokens_ref[...]

    def remote(index, part, owner, to):
        piece = out_ref.at[part, at(owner)]
        return pltpu.make_async_remote_copy(
            src_ref=piece, dst_ref=piece,
            send_sem=send_sem.at[index], recv_sem=recv_sem.at[index],
            device_id={"chan": to}, device_id_type=MESH,
        )

    copies = [
        remote(0, every, me, mate),
        remote(1, low, me, beside),
        remote(2, high, me, beside),
        remote(3, high, me, above),
        remote(4, low, me, above),
        remote(5, low, beside, above),
        remote(6, high, above, beside),
        remote(7, every, beside, mate),
        remote(8, every, above, mate),
        remote(9, low, opposite, mate),
        remote(10, high, opposite, mate),
    ]

    def permute(block, initial):
        def tile(column, carry):
            partner = partner_ref[:, at(column)]
            part = jnp.zeros((rows, cols), F32)
            for owner in (block, flip(block, 1)):
                start = pl.multiple_of(owner * cols, cols)
                part += jnp.dot(
                    out_ref[:rows, pl.ds(start, cols)],
                    chosen_deep(partner, start, cols),
                    preferred_element_type=F32,
                )
            if not initial:
                part += out_ref[rows:, at(column)].astype(F32)
            out_ref[rows:, at(column)] = part.astype(BF16)
            return carry

        lax.fori_loop(0, width // cols, tile, 0)

    for index in (1, 3, 0, 2, 4):
        copies[index].start()
    copies[0].wait_recv()
    permute(me, True)
    for arrived, onward in ((1, 5), (3, 6), (2, 7), (4, 8)):
        copies[arrived].wait_recv()
        copies[onward].start()
    copies[7].wait_recv()
    permute(beside, False)
    for arrived, onward in ((5, 9), (6, 10)):
        copies[arrived].wait_recv()
        copies[onward].start()
    copies[8].wait_recv()
    permute(above, False)
    copies[9].wait_recv()
    copies[10].wait_recv()
    permute(opposite, False)
    for copy in copies:
        copy.wait_send()


def gather_both(tokens, partner):
    rows, width = tokens.shape[0], partner.shape[1]
    vmem = pl.BlockSpec(memory_space=pltpu.VMEM)
    return pl.pallas_call(
        gather_body,
        in_specs=[vmem] * 2,
        out_specs=vmem,
        out_shape=jax.ShapeDtypeStruct((2 * rows, width), BF16),
        scratch_shapes=[pltpu.SemaphoreType.DMA((11,)), pltpu.SemaphoreType.DMA((11,))],
        compiler_params=pltpu.CompilerParams(
            collective_id=3, has_side_effects=True, vmem_limit_bytes=VMEM_LIMIT
        ),
        cost_estimate=pl.CostEstimate(
            flops=2 * rows * width * width, bytes_accessed=6 * rows * width, transcendentals=0
        ),
    )(tokens, partner)


def product_body(counts, a_ref, *refs):
    step = pl.program_id(0)
    begin = 0
    for index, count in enumerate(counts):
        weight_ref, out_ref = refs[index], refs[len(counts) + index]

        @pl.when((step >= begin) & (step < begin + count))
        def _(weight_ref=weight_ref, out_ref=out_ref):
            out_ref[...] = jnp.dot(
                a_ref[...], weight_ref[...], preferred_element_type=F32
            ).astype(BF16)

        begin += count


def products(a, weights):
    rows, depth = a.shape
    counts = tuple(w.shape[1] // TILE for w in weights)
    steps = sum(counts)

    def tile_of(index):
        begin = sum(counts[:index])
        return lambda j: (0, jnp.clip(j - begin, 0, counts[index] - 1))

    return pl.pallas_call(
        functools.partial(product_body, counts),
        grid=(steps,),
        in_specs=[pl.BlockSpec((rows, depth), lambda j: (0, 0))]
        + [pl.BlockSpec((depth, TILE), tile_of(i)) for i in range(len(weights))],
        out_specs=[pl.BlockSpec((rows, TILE), tile_of(i)) for i in range(len(weights))],
        out_shape=[jax.ShapeDtypeStruct((rows, w.shape[1]), BF16) for w in weights],
        compiler_params=params(1),
        cost_estimate=pl.CostEstimate(
            flops=2 * rows * depth * TILE * steps,
            bytes_accessed=2 * (rows * depth + (depth + rows) * TILE * steps),
            transcendentals=0,
        ),
    )(a, *weights)


def silu(v):
    return 0.5 * v * (1.0 + jnp.tanh(0.5 * v))


def column_of(values, head):
    lanes = lax.broadcasted_iota(jnp.int32, values.shape, 1)
    return jnp.sum(jnp.where(lanes == head, values, 0.0), axis=1, keepdims=True)


def state_body(value_ref, halo_ref, taps_ref, b_ref, weight_ref, grown_ref, xs_ref, state_ref):
    branch, head = pl.program_id(0), pl.program_id(1)
    rows = value_ref.shape[0]
    nstate = b_ref.shape[1]
    value = value_ref[...].astype(F32)
    halo = halo_ref[...].astype(F32)
    weight = column_of(weight_ref[...], head)

    def finish(conv, last):
        decay = column_of(grown_ref[last : last + 1, :], head)
        xs = silu(conv).astype(BF16)
        xs_ref[...] = xs
        weighted = (xs.astype(F32) * weight).astype(BF16)
        state = lax.dot_general(
            b_ref[...], weighted, (((0,), (0,)), ((), ())), preferred_element_type=F32
        )
        state_ref[0, 0, :nstate, :] = state.astype(BF16)
        state_ref[0, 0, nstate:, :] = jnp.broadcast_to(decay, (HALO, state.shape[1])).astype(BF16)

    @pl.when(branch == 0)
    def _():
        ext = jnp.concatenate([halo, value], axis=0)
        conv = taps_ref[KW - 1 : KW, :] * value
        for k in range(KW - 1):
            low = HALO - (KW - 1) + k
            conv += taps_ref[k : k + 1, :] * ext[low : low + rows]
        finish(conv, rows - 1)

    @pl.when(branch == 1)
    def _():
        ext = jnp.concatenate([value, halo], axis=0)
        conv = taps_ref[KW - 1 : KW, :] * value
        for k in range(KW - 1):
            low = KW - 1 - k
            conv += taps_ref[k : k + 1, :] * ext[low : low + rows]
        finish(conv, 0)


def step_body(raw_ref, bias_ref, rate_ref, step_ref, cum_ref, weight_ref, grown_ref):
    rows = raw_ref.shape[0] // 2
    order = lax.broadcasted_iota(jnp.int32, (rows, rows), 0) - lax.broadcasted_iota(
        jnp.int32, (rows, rows), 1
    )
    for branch in (0, 1):
        part = pl.ds(branch * rows, rows)
        raw = raw_ref[part, :] + bias_ref[...]
        step = jnp.maximum(raw, 0.0) + jnp.log1p(jnp.exp(-jnp.abs(raw)))
        summed = jnp.where(order >= 0 if branch == 0 else order <= 0, 1.0, 0.0)
        step_ref[part, :] = step
        cum = jnp.dot(
            summed,
            -step * rate_ref[...],
            precision=lax.Precision.HIGHEST,
            preferred_element_type=F32,
        )
        end = cum[rows - 1 : rows] if branch == 0 else cum[0:1]
        cum_ref[part, :] = cum
        weight_ref[part, :] = jnp.exp(end - cum) * step
        grown_ref[part, :] = jnp.exp(cum)


def scan_body(
    skip_ref, packed_ref, xs_ref, bc_ref, cum_ref, grown_ref, step_row_ref, cum_row_ref, gate_ref, gain_ref,
    out_ref, scores, local, inbox, outbox, send_sem, recv_sem,
):
    heads = packed_ref.shape[1]
    nstate, head_dim = inbox.shape[2:]
    rows = out_ref.shape[0]
    size = min(TILE, rows)
    count = lax.axis_size("seq")
    place = lax.axis_index("seq")
    toward = [(place + 1) % count, (place + count - 1) % count]
    first = [place == 0, place == count - 1]
    last = [place == count - 1, place == 0]

    barrier = pltpu.get_barrier_semaphore()
    for branch in (0, 1):

        @pl.when(jnp.logical_not(last[branch]))
        def _(branch=branch):
            pl.semaphore_signal(
                barrier, inc=1, device_id={"seq": toward[branch]}, device_id_type=MESH
            )

    pl.semaphore_wait(barrier, jnp.where(place == 0, 0, 1) + jnp.where(place == count - 1, 0, 1))

    def copy(branch, head):
        return pltpu.make_async_remote_copy(
            src_ref=outbox.at[branch, head],
            dst_ref=inbox.at[branch, head],
            send_sem=send_sem.at[branch, head],
            recv_sem=recv_sem.at[branch, head],
            device_id={"seq": toward[branch]},
            device_id_type=MESH,
        )

    def relay(branch, head):
        copy(branch, head).wait_recv()

        @pl.when(jnp.logical_not(last[branch]))
        def _():
            decay = packed_ref[branch, head, nstate : nstate + 1, :].astype(F32)
            end = packed_ref[branch, head, :nstate, :].astype(F32)
            arrived = inbox[branch, head].astype(F32)
            outbox[branch, head] = (decay * arrived + end).astype(BF16)
            copy(branch, head).start()

    def lanes(head):
        return pl.ds(pl.multiple_of(head * head_dim, head_dim), head_dim)

    def within(branch):
        base = branch * rows
        part = pl.ds(base, rows)
        scores[...] = lax.dot_general(
            bc_ref[part, nstate:],
            bc_ref[part, :nstate],
            (((1,), (1,)), ((), ())),
            preferred_element_type=F32,
        )
        sign = 1 - 2 * branch
        below = lax.broadcasted_iota(jnp.int32, (size, size), 0) - lax.broadcasted_iota(
            jnp.int32, (size, size), 1
        )

        def one(head, carry):
            cum = column_of(cum_ref[part, :], head)
            cum_row = cum_row_ref[branch * heads + head]
            step_row = step_row_ref[branch * heads + head]
            skip = skip_ref[head]
            xs = xs_ref[part, lanes(head)]
            for t in range(0, rows, size):
                at = slice(t, t + size)
                total = xs[at].astype(F32) * skip
                for s in range(0, rows, size):
                    if sign * (t - s) < 0:
                        continue
                    gaps = cum[at] - cum_row[:, s : s + size]
                    if s == t:
                        gaps = jnp.where(sign * below >= 0, gaps, -jnp.inf)
                    mixing = jnp.exp(gaps) * (scores[at, s : s + size] * step_row[:, s : s + size])
                    total += jnp.dot(
                        mixing.astype(BF16), xs[s : s + size], preferred_element_type=F32
                    )
                local[base + t : base + t + size, lanes(head)] = total
            return carry

        lax.fori_loop(0, heads, one, 0)

    def normalize(branch):
        part = pl.ds(branch * rows, rows)

        def one(head, carry):
            grown = column_of(grown_ref[part, :], head)
            carried = jnp.dot(
                bc_ref[part, nstate:], inbox[branch, head], preferred_element_type=F32
            )
            y = local[part, lanes(head)] + grown * carried
            gated = y * silu(gate_ref[part, lanes(head)].astype(F32))
            mean = jnp.mean(gated * gated, axis=1, keepdims=True)
            normed = gated * lax.rsqrt(mean + 1e-05) * gain_ref[:, lanes(head)]
            out_ref[:, lanes(branch * heads + head)] = normed.astype(BF16)
            return carry

        lax.fori_loop(0, heads, one, 0)

    for branch in (0, 1):

        @pl.when(first[branch])
        def _(branch=branch):
            for head in range(heads):
                inbox[branch, head] = jnp.zeros(inbox.shape[2:], BF16)
                outbox[branch, head] = packed_ref[branch, head, :nstate, :]
                copy(branch, head).start()

    def relays(near, branch):
        @pl.when(near & jnp.logical_not(first[branch]))
        def _():
            for head in range(heads):
                relay(branch, head)

    forward_near, reverse_near = 2 * place < count, 2 * place >= count
    relays(forward_near, 0)
    relays(reverse_near, 1)
    within(0)
    relays(forward_near, 1)
    relays(reverse_near, 0)
    within(1)
    normalize(0)
    normalize(1)

    for branch in (0, 1):

        @pl.when(jnp.logical_not(last[branch]))
        def _(branch=branch):
            for head in range(heads):
                copy(branch, head).wait_send()


def shift(block, distance):
    count = lax.axis_size("seq")
    route = [(i, i + distance) for i in range(count) if 0 <= i + distance < count]
    return lax.ppermute(block, "seq", route)


def flip(me, bit):
    return me + bit * (1 - 2 * ((me // bit) % 2))


def greet(partners):
    barrier = pltpu.get_barrier_semaphore()
    for partner in partners:
        pl.semaphore_signal(barrier, inc=1, device_id={"chan": partner}, device_id_type=MESH)
    pl.semaphore_wait(barrier, len(partners))


def output_body(
    normed_ref, table_ref, partner_ref, out_ref,
    reverse, total, mine, theirs, sent, diagonal, across,
    core_send, core_recv, chip_send, chip_recv,
):
    rows, width = reverse.shape
    inner = table_ref.shape[0]
    cols = out_ref.shape[1]
    half = rows // 2
    me = lax.axis_index("chan")
    mate, beside, above = flip(me, 1), flip(me, 2), flip(me, 4)
    greet((mate, beside, above))

    def at(block):
        return pl.ds(pl.multiple_of(block * cols, cols), cols)

    def project(block, carry):
        reverse[:, at(block)] = jnp.dot(
            normed_ref[:, inner:], table_ref[:, at(block)], preferred_element_type=F32
        ).astype(BF16)
        return carry

    lax.fori_loop(0, width // cols, project, 0)

    def remote(src, dst, send_sem, recv_sem, to):
        return pltpu.make_async_remote_copy(
            src_ref=src, dst_ref=dst, send_sem=send_sem, recv_sem=recv_sem,
            device_id={"chan": to}, device_id_type=MESH,
        )

    def core_copy(slot):
        return remote(
            mine.at[slot], theirs.at[slot], core_send.at[slot], core_recv.at[slot], mate
        )

    low, high = pl.ds(0, half), pl.ds(half, half)
    chip_copies = [
        remote(sent.at[0, low], diagonal.at[0], chip_send.at[0], chip_recv.at[0], beside),
        remote(sent.at[0, high], diagonal.at[1], chip_send.at[1], chip_recv.at[1], above),
        remote(sent.at[1, low], across.at[0, low], chip_send.at[2], chip_recv.at[2], beside),
        remote(sent.at[1, high], across.at[0, high], chip_send.at[3], chip_recv.at[3], beside),
        remote(sent.at[2, high], across.at[1, high], chip_send.at[4], chip_recv.at[4], above),
        remote(sent.at[2, low], across.at[1, low], chip_send.at[5], chip_recv.at[5], above),
    ]

    def stage(chip, carry):
        is_beside = (chip == 0) | (chip == 1)
        is_above = (chip == 0) | (chip == 2)
        base = jnp.where(is_beside, beside - me, 0) + jnp.where(is_above, above - me, 0) + me

        def compute(turn, inner_carry):
            block = jnp.where(turn == 0, flip(base, 1), base)
            partner = partner_ref[:, at(block)]
            part = jnp.dot(
                normed_ref[:, :inner], table_ref[:, at(block)], preferred_element_type=F32
            )
            deep = min(4 * DEPTH, width)
            for depth in range(0, width, deep):
                part += jnp.dot(
                    reverse[:, depth : depth + deep],
                    chosen_deep(partner, depth, deep),
                    preferred_element_type=F32,
                )
            total[...] = part

            @pl.when(turn == 0)
            def _():
                mine[chip] = part.astype(BF16)
                core_copy(chip).start()

            return inner_carry

        lax.fori_loop(0, 2, compute, 0)
        core_copy(chip).wait_recv()
        total[...] += theirs[chip].astype(F32)

        @pl.when(chip == 0)
        def _():
            sent[0] = total[...].astype(BF16)
            chip_copies[0].start()
            chip_copies[1].start()

        @pl.when(chip == 1)
        def _():
            sent[1, :half] = total[:half].astype(BF16)
            chip_copies[2].start()
            chip_copies[1].wait_recv()
            sent[1, half:] = (total[half:] + diagonal[1].astype(F32)).astype(BF16)
            chip_copies[3].start()

        @pl.when(chip == 2)
        def _():
            sent[2, half:] = total[half:].astype(BF16)
            chip_copies[4].start()
            chip_copies[0].wait_recv()
            sent[2, :half] = (total[:half] + diagonal[0].astype(F32)).astype(BF16)
            chip_copies[5].start()

        return carry

    lax.fori_loop(0, 4, stage, 0)
    for copy in chip_copies[2:]:
        copy.wait_recv()
    out_ref[...] = total[...] + across[0].astype(F32) + across[1].astype(F32)
    for slot in range(4):
        core_copy(slot).wait_send()
    for copy in chip_copies:
        copy.wait_send()


def output_sum(normed, table, partner, cols):
    rows = normed.shape[0]
    width = table.shape[1]
    vmem = pl.BlockSpec(memory_space=pltpu.VMEM)
    block = (rows, cols)
    return pl.pallas_call(
        output_body,
        in_specs=[vmem] * 3,
        out_specs=vmem,
        out_shape=jax.ShapeDtypeStruct(block, F32),
        scratch_shapes=[
            pltpu.VMEM((rows, width), BF16),
            pltpu.VMEM(block, F32),
            pltpu.VMEM((4,) + block, BF16),
            pltpu.VMEM((4,) + block, BF16),
            pltpu.VMEM((3,) + block, BF16),
            pltpu.VMEM((2, rows // 2, cols), BF16),
            pltpu.VMEM((2,) + block, BF16),
            pltpu.SemaphoreType.DMA((4,)),
            pltpu.SemaphoreType.DMA((4,)),
            pltpu.SemaphoreType.DMA((6,)),
            pltpu.SemaphoreType.DMA((6,)),
        ],
        compiler_params=pltpu.CompilerParams(
            collective_id=2, has_side_effects=True, vmem_limit_bytes=VMEM_LIMIT
        ),
        cost_estimate=pl.CostEstimate(
            flops=2 * rows * width * (2 * table.shape[0] + width),
            bytes_accessed=2 * table.size + 2 * normed.size,
            transcendentals=0,
        ),
    )(normed, table, partner)


def shards(
    tokens,
    gate_proj,
    value_proj,
    state_proj,
    step_proj,
    step_bias,
    decay_rate,
    skip_gain,
    conv_kernel,
    norm_gain,
    out_proj,
    complement,
    keep_mask,
):
    rows = tokens.shape[0]
    inner = gate_proj.shape[1]
    heads = step_proj.shape[1]
    head_dim = inner // heads
    nstate = state_proj.shape[1] // 2
    partner = complement[None, :]

    both = gather_both(tokens, partner)
    value, bc = products(both, (value_proj, state_proj))
    halo = jnp.concatenate(
        [shift(value[rows - HALO : rows], 1), shift(value[rows : rows + HALO], -1)], axis=0
    )
    step_raw = jnp.dot(both, step_proj, preferred_element_type=F32)
    per_step = jax.ShapeDtypeStruct((2 * rows, heads), F32)
    step, cum, weight, grown = pl.pallas_call(
        step_body, out_shape=[per_step] * 4, compiler_params=params(0)
    )(step_raw, step_bias[None, :], decay_rate[None, :])

    def as_rows(a):
        return jnp.swapaxes(a.reshape(2, rows, heads), 1, 2).reshape(2 * heads, 1, rows)

    step_rows, cum_rows = as_rows(step), as_rows(cum)
    (gate,) = products(both, (gate_proj,))

    grid = (2, heads)
    block = pl.BlockSpec((rows, head_dim), lambda b, h: (b, h))
    b_block = pl.BlockSpec((rows, nstate), lambda b, h: (b, 0))
    column = pl.BlockSpec((rows, heads), lambda b, h: (b, 0))

    xs, packed = pl.pallas_call(
        state_body,
        grid=grid,
        in_specs=[
            block,
            pl.BlockSpec((HALO, head_dim), lambda b, h: (b, h)),
            pl.BlockSpec((KW, head_dim), lambda b, h: (0, h)),
            b_block,
            column,
            column,
        ],
        out_specs=[
            block,
            pl.BlockSpec((1, 1, nstate + HALO, head_dim), lambda b, h: (b, h, 0, 0)),
        ],
        out_shape=[
            jax.ShapeDtypeStruct((2 * rows, inner), BF16),
            jax.ShapeDtypeStruct((2, heads, nstate + HALO, head_dim), BF16),
        ],
        compiler_params=params(2),
    )(value, halo, conv_kernel, bc, weight, grown)

    vmem = pl.BlockSpec(memory_space=pltpu.VMEM)
    states = (2, heads, nstate, head_dim)
    normed = pl.pallas_call(
        scan_body,
        in_specs=[pl.BlockSpec(memory_space=pltpu.SMEM)] + [vmem] * 9,
        out_specs=vmem,
        out_shape=jax.ShapeDtypeStruct((rows, 2 * inner), BF16),
        scratch_shapes=[
            pltpu.VMEM((rows, rows), F32),
            pltpu.VMEM((2 * rows, inner), F32),
            pltpu.VMEM(states, BF16),
            pltpu.VMEM(states, BF16),
            pltpu.SemaphoreType.DMA((2, heads)),
            pltpu.SemaphoreType.DMA((2, heads)),
        ],
        compiler_params=pltpu.CompilerParams(
            collective_id=1, has_side_effects=True, vmem_limit_bytes=VMEM_LIMIT
        ),
        cost_estimate=pl.CostEstimate(
            flops=8 * rows * rows * inner,
            bytes_accessed=16 * rows * inner,
            transcendentals=2 * heads * rows * rows,
        ),
    )(skip_gain, packed, xs, bc, cum, grown, step_rows, cum_rows, gate, norm_gain[None, :])

    summed = output_sum(normed, out_proj, partner, tokens.shape[1])
    return (summed * keep_mask.astype(F32) * (1.0 / 0.9)).astype(BF16)


def solution(mesh):
    return jax.shard_map(
        shards,
        mesh=mesh,
        in_specs=(
            P("seq", "chan"),
            P(None, "chan"),
            P(None, "chan"),
            P(),
            P(None, "chan"),
            P("chan"),
            P("chan"),
            P("chan"),
            P(None, "chan"),
            P("chan"),
            P("chan", None),
            P(),
            P("seq", "chan"),
        ),
        out_specs=P("seq", "chan"),
        check_vma=False,
    )
```
